32 devices in a mesh: seq: 16 (over z, x, core), batch: 2 (over y).
Axes of the slice: x: 2, y: 2, z: 4, core: 2. Of those that a mesh axis runs over, the one named last changes fastest.
Arguments:
- bases: int32 [16384, 128], P(('batch', 'seq')), parts along dimension 0, may hold values from 0 to 3
- embed_table: bfloat16 [512, 768], replicated, may hold values from -0.5 to 0.5
- norm_gains: float32 [3, 768], replicated, may hold values from 0.1 to 1.9
- depth_taps: float32 [3, 5, 768], replicated, may hold values from -2.5 to 2.5
- point_weight: bfloat16 [3, 768, 768], replicated, may hold values from -0.21875 to 0.21875
- query_weight: bfloat16 [768, 128], replicated, may hold values from -0.5390625 to 0.5390625
- key_weight: bfloat16 [768, 128], replicated, may hold values from -0.5390625 to 0.5390625
- pair_kernel: bfloat16 [3, 3, 128, 128], replicated, may hold values from -0.1875 to 0.1875
Outputs:
- trunk: bfloat16 [16384, 768], P(('batch', 'seq')), parts along dimension 0
- pair_map: bfloat16 [1024, 512, 128], P(('batch', 'seq')), parts along dimension 0
The draws below stay inside these ranges and needn't reach their ends.
There are 2 independent parts, one for each index of `batch`. The reference program is written for one: setup_inputs(seed, part) draws one part's arguments, and reference() takes and returns one part's arrays. A program takes and returns all parts, laid end to end along the dimension named above; an argument that names none is the same for every part. Nothing has to cross between parts.
All inputs are finite; a program needn't handle non-finite values.
Results may differ from the reference program's by a relative error of at most 0.018.
Values may be sent and summed in bfloat16 or wider, within the bound.
A program may use at most 128 MiB of HBM per device.

```python
import jax
import jax.numpy as jnp
from jax import lax

C = 768
PC = 128
BASES = 128
KW = 5
FIRST_DILATION = 2
SECOND_DILATION = 8
THIRD_DILATION = 32
POOL = 16
BINS = 8192


def with_ends(array, own_key, low, high):
    shape = array.shape
    place = [jax.random.randint(jax.random.fold_in(own_key, axis), (), 0, shape[axis]) for axis in range(len(shape))]
    array = array.at[tuple(place)].set(low)
    longest = shape.index(max(shape))
    place[longest] = (place[longest] + 1) % shape[longest]
    return array.at[tuple(place)].set(high)


def bell_draw(key, dims, spread, most, kind=jnp.bfloat16):
    entries = spread * jax.random.normal(key, dims, jnp.float32)
    return jnp.clip(entries, min=-most, max=most).astype(kind)


def setup_inputs(seed: int = 0, part: int = 0) -> dict:
    key_of = jax.random.split(jax.random.key(seed), 9)
    part_splits = jax.random.split(jax.random.fold_in(key_of[8], part), 9)
    bases = with_ends(jax.random.randint(part_splits[0], (BINS, BASES), 0, 4), jax.random.fold_in(part_splits[0], 1), 0, 3).astype(jnp.int32)
    embed_table = bell_draw(key_of[1], (4 * BASES, C), BASES ** -0.5, 0.5)
    norm_gains = jnp.clip(1.0 + 0.18 * jax.random.normal(key_of[2], (3, C), jnp.float32), 0.1, 1.9)
    depth_taps = bell_draw(key_of[3], (3, KW, C), KW ** -0.5, 2.5, jnp.float32)
    point_weight = bell_draw(key_of[4], (3, C, C), C ** -0.5, 0.21875)
    query_weight = bell_draw(key_of[5], (C, PC), (2.5 / C ** 0.5), 0.5390625)
    key_weight = bell_draw(key_of[6], (C, PC), (2.5 / C ** 0.5), 0.5390625)
    pair_kernel = bell_draw(key_of[7], (3, 3, PC, PC), (9 * PC) ** -0.5, 0.1875)
    return dict(bases=bases, embed_table=embed_table, norm_gains=norm_gains, depth_taps=depth_taps, point_weight=point_weight, query_weight=query_weight, key_weight=key_weight, pair_kernel=pair_kernel)


def embed_bases(bases, embed_table):
    one_hot_bases = (bases[:, :, None] == jnp.arange(4, dtype=jnp.int32)).astype(jnp.bfloat16)
    one_hot_bases = one_hot_bases.reshape(bases.shape[0], -1)
    return jnp.dot(one_hot_bases, embed_table, preferred_element_type=jnp.float32).astype(jnp.bfloat16)

def normalize(value_rows, gain):
    floats = value_rows.astype(jnp.float32)
    scale = lax.rsqrt(lax.optimization_barrier(jnp.mean(floats * floats, axis=-1, keepdims=True)) + 1e-06)
    return (floats * scale * gain).astype(jnp.bfloat16)

def mix_rows(inner, normed, taps, point, dilation_reach, rows):
    summed = jnp.zeros((rows, normed.shape[1]), jnp.float32)
    for offset in range(KW):
        summed = summed + normed[offset * dilation_reach:offset * dilation_reach + rows].astype(jnp.float32) * taps[offset]
    activated = jax.nn.gelu(summed).astype(jnp.bfloat16)
    return (inner.astype(jnp.float32) + jnp.dot(activated, point, preferred_element_type=jnp.float32)).astype(jnp.bfloat16)

def pair_conv(extended, pair_kernel, rows, width):
    padded = jnp.pad(extended, ((0, 0), (1, 1), (0, 0)))
    channels = extended.shape[2]
    summed = jnp.zeros((rows * width, channels), jnp.float32)
    for row_tap in range(3):
        for col_tap in range(3):
            window = padded[row_tap:row_tap + rows, col_tap:col_tap + width].reshape(rows * width, channels)
            summed = summed + jnp.dot(window, pair_kernel[row_tap, col_tap], preferred_element_type=jnp.float32)
    center = extended[1:rows + 1].astype(jnp.float32).reshape(rows * width, channels)
    return (center + jax.nn.gelu(summed)).astype(jnp.bfloat16).reshape(rows, width, channels)

def reference(bases, embed_table, norm_gains, depth_taps, point_weight, query_weight, key_weight, pair_kernel):
    current = embed_bases(bases, embed_table)
    total = current.shape[0]
    for trunk_layer, dilation_reach in enumerate((FIRST_DILATION, SECOND_DILATION, THIRD_DILATION)):
        normed = normalize(current, norm_gains[trunk_layer])
        padded = jnp.pad(normed, ((2 * dilation_reach, 2 * dilation_reach), (0, 0)))
        current = mix_rows(current, padded, depth_taps[trunk_layer], point_weight[trunk_layer], dilation_reach, total)
    trunk = current
    pooled = lax.optimization_barrier(jnp.mean(trunk.astype(jnp.float32).reshape(-1, POOL, trunk.shape[1]), axis=1)).astype(jnp.bfloat16)
    queries = jnp.dot(pooled, query_weight, preferred_element_type=jnp.float32).astype(jnp.bfloat16)
    keys = jnp.dot(pooled, key_weight, preferred_element_type=jnp.float32).astype(jnp.bfloat16)
    pair = (queries.astype(jnp.float32)[:, None, :] * keys.astype(jnp.float32)[None, :, :]).astype(jnp.bfloat16)
    extended = jnp.pad(pair, ((1, 1), (0, 0), (0, 0)))
    pair_map = pair_conv(extended, pair_kernel, pair.shape[0], pair.shape[1])
    return (trunk, pair_map)
```

```python
import functools

import jax
import jax.numpy as jnp
from jax import lax
from jax.experimental import pallas as pl
from jax.experimental.pallas import tpu as pltpu
from jax.sharding import PartitionSpec as P

KW = 5
DILATIONS = (2, 8, 32)
POOL = 16
HALO = 96
CHUNK = 32
GELU_A = 0.7978845608028654
GELU_B = 0.7978845608028654 * 0.044715
MESH = pl.DeviceIdType.MESH
F32 = jnp.float32
BF16 = jnp.bfloat16


def gelu(v):
    half = 0.5 * v
    return half + half * jnp.tanh(v * (GELU_A + GELU_B * (v * v)))


def trunk_kernel(
    n,
    bases,
    table,
    gains,
    taps,
    point,
    query_w,
    key_w,
    trunk_out,
    kq,
    base_v,
    table_v,
    gains_v,
    taps_v,
    point_v,
    qw_v,
    kw_v,
    hot,
    xs,
    nrm,
    act,
    trunk_v,
    local_sem,
    halo_send,
    halo_recv,
    send_sem,
    recv_sem,
):
    slab = bases.shape[0]
    channels = table.shape[1]
    full = slab + 2 * HALO
    pool_rows = slab // POOL
    me = lax.axis_index("seq")
    right = lax.rem(me + 1, n)
    left = lax.rem(me + n - 1, n)

    barrier = pltpu.get_barrier_semaphore()
    for d in range(1, n):
        pl.semaphore_signal(
            barrier, inc=1, device_id={"seq": lax.rem(me + d, n)}, device_id_type=MESH
        )

    own = pltpu.make_async_copy(bases, base_v.at[pl.ds(HALO, slab)], local_sem.at[0])
    own.start()
    get_table = pltpu.make_async_copy(table, table_v, local_sem.at[1])
    get_table.start()
    get_gains = pltpu.make_async_copy(gains, gains_v, local_sem.at[2])
    get_gains.start()
    get_taps = pltpu.make_async_copy(taps, taps_v, local_sem.at[3])
    get_taps.start()
    get_point = []
    for layer in range(3):
        get_point.append(
            pltpu.make_async_copy(point.at[layer], point_v.at[layer], local_sem.at[4 + layer])
        )
        get_point[-1].start()
    get_qw = pltpu.make_async_copy(query_w, qw_v, local_sem.at[7])
    get_qw.start()
    get_kw = pltpu.make_async_copy(key_w, kw_v, local_sem.at[8])
    get_kw.start()

    pl.semaphore_wait(barrier, n - 1)
    to_right = pltpu.make_async_remote_copy(
        src_ref=bases.at[pl.ds(slab - HALO, HALO)],
        dst_ref=base_v.at[pl.ds(0, HALO)],
        send_sem=halo_send.at[0],
        recv_sem=halo_recv.at[0],
        device_id={"seq": right},
        device_id_type=MESH,
    )
    to_right.start()
    to_left = pltpu.make_async_remote_copy(
        src_ref=bases.at[pl.ds(0, HALO)],
        dst_ref=base_v.at[pl.ds(HALO + slab, HALO)],
        send_sem=halo_send.at[1],
        recv_sem=halo_recv.at[1],
        device_id={"seq": left},
        device_id_type=MESH,
    )
    to_left.start()

    width = table.shape[0]
    places = width // 4
    spread = (
        lax.broadcasted_iota(jnp.int32, (places, width), 1) // 4
        == lax.broadcasted_iota(jnp.int32, (places, width), 0)
    ).astype(BF16)

    def embed(start, rows):
        codes = base_v[pl.ds(start, rows), :].astype(F32).astype(BF16)
        wide = jnp.dot(codes, spread, preferred_element_type=F32)
        letter = (lax.broadcasted_iota(jnp.int32, (rows, width), 1) % 4).astype(F32)
        hot[pl.ds(start, rows), :] = jnp.where(wide == letter, 1.0, 0.0).astype(BF16)
        for col in range(0, channels, 256):
            xs[pl.ds(start, rows), pl.ds(col, 256)] = jnp.dot(
                hot[pl.ds(start, rows), :],
                table_v[:, pl.ds(col, 256)],
                preferred_element_type=F32,
            )

    own.wait()
    get_table.wait()
    embed(HALO, slab)
    to_right.wait()
    to_left.wait()
    embed(0, HALO)
    embed(HALO + slab, HALO)
    get_gains.wait()
    get_taps.wait()

    first_row = me * slab - HALO
    last_row = n * slab
    reaches = [2 * s for s in DILATIONS]
    for layer, s in enumerate(DILATIONS):
        out_lo = HALO - sum(reaches[layer + 1 :])
        out_rows = full - 2 * out_lo
        in_lo = (out_lo - reaches[layer]) // CHUNK * CHUNK
        in_rows = full - 2 * in_lo

        def norm_step(i, _, in_lo=in_lo):
            r = pl.multiple_of(in_lo + i * CHUNK, CHUNK)
            rows = xs[pl.ds(r, CHUNK), :]
            mean = jnp.sum(rows * rows, axis=1, keepdims=True) * (1.0 / channels)
            place = first_row + r + lax.broadcasted_iota(jnp.int32, (CHUNK, 1), 0)
            inside = jnp.logical_and(place >= 0, place < last_row)
            scale = jnp.where(inside, lax.rsqrt(mean + 1e-6), 0.0)
            nrm[pl.ds(r, CHUNK), :] = rows * scale
            return 0

        lax.fori_loop(0, in_rows // CHUNK, norm_step, 0)

        scaled = taps_v[layer] * gains_v[pl.ds(layer, 1), :]

        def conv_step(i, _, out_lo=out_lo, s=s, scaled=scaled):
            r = i * CHUNK
            for col in range(0, channels, 128):
                total = None
                if s % 8:
                    low = (out_lo - 2 * s) // 8 * 8
                    lead = out_lo - 2 * s - low
                    span = -(-(lead + CHUNK + 4 * s) // 8) * 8
                    near = nrm[pl.ds(pl.multiple_of(r + low, 8), span), pl.ds(col, 128)]
                for t in range(KW):
                    if s % 8:
                        part = near[lead + t * s : lead + t * s + CHUNK]
                    else:
                        place = pl.multiple_of(r + (out_lo + (t - 2) * s), 8)
                        part = nrm[pl.ds(place, CHUNK), pl.ds(col, 128)]
                    term = part * scaled[t : t + 1, col : col + 128]
                    total = term if total is None else total + term
                act[pl.ds(pl.multiple_of(r, CHUNK), CHUNK), pl.ds(col, 128)] = gelu(total).astype(
                    BF16
                )
            return 0

        lax.fori_loop(0, out_rows // CHUNK, conv_step, 0)

        get_point[layer].wait()
        for col in range(0, channels, 256):
            mixed = xs[pl.ds(out_lo, out_rows), pl.ds(col, 256)] + jnp.dot(
                act[pl.ds(0, out_rows), :],
                point_v[layer, :, pl.ds(col, 256)],
                preferred_element_type=F32,
            )
            if layer < 2:
                xs[pl.ds(out_lo, out_rows), pl.ds(col, 256)] = mixed
            else:
                trunk_v[:, pl.ds(col, 256)] = mixed.astype(BF16)

    put_trunk = pltpu.make_async_copy(trunk_v, trunk_out, local_sem.at[9])
    put_trunk.start()
    group = lax.broadcasted_iota(jnp.int32, (pool_rows, slab), 1) // POOL
    pooler = jnp.where(
        group == lax.broadcasted_iota(jnp.int32, (pool_rows, slab), 0), 1.0 / POOL, 0.0
    ).astype(BF16)
    pooled = jnp.dot(pooler, trunk_v[...], preferred_element_type=F32).astype(BF16)
    get_qw.wait()
    get_kw.wait()
    mine = pl.ds(pl.multiple_of(me * pool_rows, pool_rows), pool_rows)
    kq[mine, 0:128] = jnp.dot(pooled, qw_v[...], preferred_element_type=F32).astype(BF16)
    kq[mine, 128:256] = jnp.dot(pooled, kw_v[...], preferred_element_type=F32).astype(BF16)

    copies = []
    for d in range(1, n):
        copies.append(
            pltpu.make_async_remote_copy(
                src_ref=kq.at[mine],
                dst_ref=kq.at[mine],
                send_sem=send_sem.at[d - 1],
                recv_sem=recv_sem.at[d - 1],
                device_id={"seq": lax.rem(me + d, n)},
                device_id_type=MESH,
            )
        )
        copies[-1].start()
    for copy in copies:
        copy.wait()
    put_trunk.wait()


def pair_kernel_body(n, block, kq, weight, trunk_in, pair_out, trunk_out, w32, keys3, keysf, qrows, qcols, sem):
    step = pl.program_id(0)
    steps = pl.num_programs(0)
    width = kq.shape[0]
    pool_rows = width // n
    me = lax.axis_index("seq")

    @pl.when(step == 0)
    def _():
        pltpu.make_async_copy(trunk_in, trunk_out, sem).start()
        w32[...] = weight[...].astype(F32)
        keys = kq[:, 128:256].astype(F32)
        keysf[...] = keys
        zero = jnp.zeros((1, 128), F32)
        keys3[:, 0:128] = jnp.concatenate([zero, keys[:-1]], axis=0).astype(BF16)
        keys3[:, 128:256] = keys.astype(BF16)
        keys3[:, 256:384] = jnp.concatenate([keys[1:], zero], axis=0).astype(BF16)
        start = me * pool_rows
        before = pl.multiple_of(jnp.maximum(start - 16, 0), 16)
        after = pl.multiple_of(jnp.minimum(start + pool_rows, width - 16), 16)
        start = pl.multiple_of(start, 16)
        above = jnp.where(me > 0, kq[pl.ds(before, 16), 0:128].astype(F32), 0.0)
        below = jnp.where(me < n - 1, kq[pl.ds(after, 16), 0:128].astype(F32), 0.0)
        middle = kq[pl.ds(start, pool_rows), 0:128].astype(F32)
        rows = jnp.concatenate(
            [above[15:16], middle, below[0:1], jnp.zeros((126 - pool_rows, 128), F32)], axis=0
        )
        qrows[...] = rows[0 : qrows.shape[0]]
        cols = rows.T
        for i in range(pool_rows + 2):
            qcols[i] = jnp.broadcast_to(cols[:, i : i + 1], (128, 128))

    for half in range(block // 2):
        base = step * block + half * 2
        kernels = []
        for k in range(2):
            parts = []
            for b in range(3):
                parts.append(
                    (
                        qcols[base + k] * w32[0, b]
                        + qcols[base + k + 1] * w32[1, b]
                        + qcols[base + k + 2] * w32[2, b]
                    ).astype(BF16)
                )
            kernels.append(jnp.concatenate(parts, axis=0))
        conv = jnp.dot(
            keys3[...], jnp.concatenate(kernels, axis=1), preferred_element_type=F32
        )
        for k in range(2):
            pair = (keysf[...] * qrows[pl.ds(base + k + 1, 1), :]).astype(BF16).astype(F32)
            pair_out[half * 2 + k] = (pair + gelu(conv[:, k * 128 : k * 128 + 128])).astype(BF16)

    @pl.when(step == steps - 1)
    def _():
        pltpu.make_async_copy(trunk_in, trunk_out, sem).wait()


def on_device(
    n, bases, embed_table, norm_gains, depth_taps, point_weight, query_weight, key_weight, pair_kernel
):
    slab = bases.shape[0]
    channels = embed_table.shape[1]
    full = slab + 2 * HALO
    pool_rows = slab // POOL
    width = pool_rows * n
    any_spec = pl.BlockSpec(memory_space=pl.ANY)
    vmem_spec = pl.BlockSpec(memory_space=pltpu.VMEM)
    trunk, kq = pl.pallas_call(
        functools.partial(trunk_kernel, n),
        out_shape=(
            jax.ShapeDtypeStruct((slab, channels), BF16),
            jax.ShapeDtypeStruct((width, 256), BF16),
        ),
        in_specs=[any_spec] * 7,
        out_specs=(any_spec, vmem_spec),
        scratch_shapes=[
            pltpu.VMEM((full, bases.shape[1]), jnp.int32),
            pltpu.VMEM(embed_table.shape, BF16),
            pltpu.VMEM(norm_gains.shape, F32),
            pltpu.VMEM(depth_taps.shape, F32),
            pltpu.VMEM(point_weight.shape, BF16),
            pltpu.VMEM(query_weight.shape, BF16),
            pltpu.VMEM(key_weight.shape, BF16),
            pltpu.VMEM((full, embed_table.shape[0]), BF16),
            pltpu.VMEM((full, channels), F32),
            pltpu.VMEM((full, channels), F32),
            pltpu.VMEM((full, channels), BF16),
            pltpu.VMEM((slab, channels), BF16),
            pltpu.SemaphoreType.DMA((10,)),
            pltpu.SemaphoreType.DMA((2,)),
            pltpu.SemaphoreType.DMA((2,)),
            pltpu.SemaphoreType.DMA((n - 1,)),
            pltpu.SemaphoreType.DMA((n - 1,)),
        ],
        compiler_params=pltpu.CompilerParams(
            collective_id=0, has_side_effects=True, vmem_limit_bytes=40 * 1024 * 1024
        ),
        name="trunk_and_gather",
    )(bases, embed_table, norm_gains, depth_taps, point_weight, query_weight, key_weight)

    block = 4
    pair_map, trunk = pl.pallas_call(
        functools.partial(pair_kernel_body, n, block),
        grid=(pool_rows // block,),
        out_shape=(
            jax.ShapeDtypeStruct((pool_rows, width, 128), BF16),
            jax.ShapeDtypeStruct((slab, channels), BF16),
        ),
        in_specs=[
            pl.BlockSpec((width, 256), lambda i: (0, 0)),
            pl.BlockSpec((3, 3, 128, 128), lambda i: (0, 0, 0, 0)),
            any_spec,
        ],
        out_specs=(pl.BlockSpec((block, width, 128), lambda i: (i, 0, 0)), any_spec),
        scratch_shapes=[
            pltpu.VMEM((3, 3, 128, 128), F32),
            pltpu.VMEM((width, 384), BF16),
            pltpu.VMEM((width, 128), F32),
            pltpu.VMEM((pool_rows + 8, 128), F32),
            pltpu.VMEM((pool_rows + 2, 128, 128), F32),
            pltpu.SemaphoreType.DMA,
        ],
        compiler_params=pltpu.CompilerParams(vmem_limit_bytes=40 * 1024 * 1024),
        name="pair_map",
    )(kq, pair_kernel, trunk)
    return (trunk, pair_map)


def solution(mesh):
    return jax.shard_map(
        functools.partial(on_device, mesh.shape["seq"]),
        mesh=mesh,
        in_specs=(P(("batch", "seq"), None), P(), P(), P(), P(), P(), P(), P()),
        out_specs=(P(("batch", "seq"), None), P(("batch", "seq"), None, None)),
        check_vma=False,
    )
```

```python
import functools

import jax
import jax.numpy as jnp
from jax import lax
from jax.experimental import pallas as pl
from jax.experimental.pallas import tpu as pltpu
from jax.sharding import PartitionSpec as P

KW = 5
DILATIONS = (2, 8, 32)
POOL = 16
HALO = 96
CHUNK = 32
GELU_A = 0.7978845608028654
GELU_B = 0.7978845608028654 * 0.044715
MESH = pl.DeviceIdType.MESH
F32 = jnp.float32
BF16 = jnp.bfloat16


def gelu(v):
    half = 0.5 * v
    return half + half * jnp.tanh(v * (GELU_A + GELU_B * (v * v)))


def blocks_of(rows):
    units = rows // 16
    sizes = [(units + 2 - k) // 3 * 16 for k in range(3)]
    return [(sum(sizes[:k]), sizes[k]) for k in range(3)]


def pieces_of(low, rows, most):
    return [(low + at, min(most, rows - at)) for at in range(0, rows, most)]


def interleave(first, second):
    count = max(len(first), len(second), 1)
    done = [0, 0]
    for k in range(count):
        for which, tasks in enumerate((first, second)):
            target = len(tasks) * (k + 1) // count
            while done[which] < target:
                tasks[done[which]]()
                done[which] += 1


def trunk_kernel(
    n,
    bases,
    table,
    gains,
    taps,
    point,
    query_w,
    key_w,
    trunk_out,
    keys,
    queries,
    base_v,
    table_v,
    gains_v,
    taps_v,
    point_v,
    qw_v,
    kw_v,
    hot,
    xs,
    nrm,
    act,
    trunk_v,
    local_sem,
    halo_send,
    halo_recv,
    query_send,
    query_recv,
    send_sem,
    recv_sem,
):
    slab = bases.shape[0]
    channels = table.shape[1]
    full = slab + 2 * HALO
    pool_rows = slab // POOL
    me = lax.axis_index("seq")
    right = lax.rem(me + 1, n)
    left = lax.rem(me + n - 1, n)

    barrier = pltpu.get_barrier_semaphore()
    for d in range(1, n):
        pl.semaphore_signal(
            barrier, inc=1, device_id={"seq": lax.rem(me + d, n)}, device_id_type=MESH
        )

    def fetch(source, target, k):
        copy = pltpu.make_async_copy(source, target, local_sem.at[k])
        copy.start()
        return copy

    own = fetch(bases, base_v.at[pl.ds(HALO, slab)], 0)
    get_table = fetch(table, table_v, 1)
    weights = [fetch(gains, gains_v, 2), fetch(taps, taps_v, 3)]
    for layer in range(3):
        weights.append(fetch(point.at[layer], point_v.at[layer], 4 + layer))
    weights.append(fetch(query_w, qw_v, 7))
    weights.append(fetch(key_w, kw_v, 8))

    width = table.shape[0]
    places = width // 4
    spread = (
        lax.broadcasted_iota(jnp.int32, (places, width), 1) // 4
        == lax.broadcasted_iota(jnp.int32, (places, width), 0)
    ).astype(BF16)
    letter = (lax.broadcasted_iota(jnp.int32, (1, width), 1) % 4).astype(F32)

    def one_hot(start, rows):
        codes = base_v[pl.ds(start, rows), :].astype(F32).astype(BF16)
        wide = jnp.dot(codes, spread, preferred_element_type=F32)
        hot[pl.ds(start, rows), :] = jnp.where(wide == letter, 1.0, 0.0).astype(BF16)

    def embed(start, rows):
        for col in range(0, channels, 256):
            xs[pl.ds(start, rows), pl.ds(col, 256)] = jnp.dot(
                hot[pl.ds(start, rows), :],
                table_v[:, pl.ds(col, 256)],
                preferred_element_type=F32,
            )

    own.wait()
    one_hot(HALO, slab)
    pl.semaphore_wait(barrier, n - 1)
    to_right = pltpu.make_async_remote_copy(
        src_ref=bases.at[pl.ds(slab - HALO, HALO)],
        dst_ref=base_v.at[pl.ds(0, HALO)],
        send_sem=halo_send.at[0],
        recv_sem=halo_recv.at[0],
        device_id={"seq": right},
        device_id_type=MESH,
    )
    to_right.start()
    to_left = pltpu.make_async_remote_copy(
        src_ref=bases.at[pl.ds(0, HALO)],
        dst_ref=base_v.at[pl.ds(HALO + slab, HALO)],
        send_sem=halo_send.at[1],
        recv_sem=halo_recv.at[1],
        device_id={"seq": left},
        device_id_type=MESH,
    )
    to_left.start()

    first_row = me * slab - HALO
    last_row = n * slab
    reaches = [2 * s for s in DILATIONS]
    lows = [HALO - sum(reaches[layer + 1 :]) for layer in range(3)]
    scaled = []

    def norm_piece(layer, r, rows):
        floats = xs[pl.ds(r, rows), :]
        mean = jnp.sum(floats * floats, axis=1, keepdims=True) * (1.0 / channels)
        scale = lax.rsqrt(mean + 1e-6)
        if r < HALO or r + rows > HALO + slab:
            place = first_row + r + lax.broadcasted_iota(jnp.int32, (rows, 1), 0)
            inside = jnp.logical_and(place >= 0, place < last_row)
            scale = jnp.where(inside, scale, 0.0)
        nrm[layer % 2, pl.ds(r, rows), :] = (floats * scale).astype(BF16)

    def norms(layer, low, rows):
        return [
            functools.partial(norm_piece, layer, r, size) for r, size in pieces_of(low, rows, 32)
        ]

    def conv_piece(layer, r, rows, col):
        s = DILATIONS[layer]
        total = None
        low = (r - 2 * s) // 16 * 16
        span = -(-(r + rows + 2 * s - low) // 16) * 16
        if s % 16:
            near = nrm[layer % 2, pl.ds(low, span), pl.ds(col, 128)]
        for t in range(KW):
            at = r + (t - 2) * s
            if s % 16:
                part = near[at - low : at - low + rows]
            else:
                part = nrm[layer % 2, pl.ds(at, rows), pl.ds(col, 128)]
            term = part * scaled[layer][t : t + 1, col : col + 128]
            total = term if total is None else total + term
        act[layer % 2, pl.ds(r, rows), pl.ds(col, 128)] = gelu(total)

    def convs(layer, k):
        at, size = blocks_of(full - 2 * lows[layer])[k]
        return [
            functools.partial(conv_piece, layer, r, rows, col)
            for r, rows in pieces_of(lows[layer] + at, size, 32)
            for col in range(0, channels, 128)
        ]

    def mix_piece(layer, r, rows, col):
        mixed = xs[pl.ds(r, rows), pl.ds(col, 256)] + jnp.dot(
            act[layer % 2, pl.ds(r, rows), :],
            point_v[layer, :, pl.ds(col, 256)],
            preferred_element_type=F32,
        )
        if layer < 2:
            xs[pl.ds(r, rows), pl.ds(col, 256)] = mixed
        else:
            trunk_v[pl.ds(r - HALO, rows), pl.ds(col, 256)] = mixed.astype(BF16)

    def mixes(layer, k):
        at, size = blocks_of(full - 2 * lows[layer])[k]
        return [
            functools.partial(mix_piece, layer, lows[layer] + at, size, col)
            for col in range(0, channels, 256)
        ]

    def next_norms(layer, k):
        if layer == 2:
            return []
        at, size = blocks_of(full - 2 * lows[layer])[k]
        return norms(layer + 1, lows[layer] + at, size)

    get_table.wait()
    for at in range(0, slab, slab // 2):
        embed(HALO + at, slab // 2)
    for task in norms(0, HALO, slab):
        task()
    to_right.wait()
    to_left.wait()
    for start in (0, HALO + slab):
        one_hot(start, HALO)
        embed(start, HALO)
    for weight in weights:
        weight.wait()
    for layer in range(3):
        scaled.append((taps_v[:, layer] * gains_v[pl.ds(layer, 1), :]).astype(BF16))
    for task in norms(0, 0, HALO) + norms(0, HALO + slab, HALO):
        task()

    interleave(convs(0, 0), [])
    for layer in range(3):
        interleave(mixes(layer, 0), convs(layer, 1))
        interleave(mixes(layer, 1), next_norms(layer, 0) + convs(layer, 2))
        following = convs(layer + 1, 0) if layer < 2 else []
        interleave(mixes(layer, 2), next_norms(layer, 1) + following)
        interleave([], next_norms(layer, 2))

    put_trunk = pltpu.make_async_copy(trunk_v, trunk_out, local_sem.at[9])
    put_trunk.start()
    group = lax.broadcasted_iota(jnp.int32, (pool_rows, slab), 1) // POOL
    pooler = jnp.where(
        group == lax.broadcasted_iota(jnp.int32, (pool_rows, slab), 0), 1.0 / POOL, 0.0
    ).astype(BF16)
    pooled = jnp.dot(pooler, trunk_v[...], preferred_element_type=F32).astype(BF16)
    mine = pl.ds(pl.multiple_of(me * pool_rows, pool_rows), pool_rows)
    keys[mine, :] = jnp.dot(pooled, kw_v[...], preferred_element_type=F32).astype(BF16)

    copies = []
    for d in sorted(range(1, n), key=lambda d: -min(d, n - d)):
        copies.append(
            pltpu.make_async_remote_copy(
                src_ref=keys.at[mine],
                dst_ref=keys.at[mine],
                send_sem=send_sem.at[d - 1],
                recv_sem=recv_sem.at[d - 1],
                device_id={"seq": lax.rem(me + d, n)},
                device_id_type=MESH,
            )
        )
        copies[-1].start()
    queries[pl.ds(16, pool_rows), :] = jnp.dot(
        pooled, qw_v[...], preferred_element_type=F32
    ).astype(BF16)
    for k, (source, target, peer) in enumerate(
        ((pool_rows, 0, right), (16, 16 + pool_rows, left))
    ):
        copies.append(
            pltpu.make_async_remote_copy(
                src_ref=queries.at[pl.ds(source, 16)],
                dst_ref=queries.at[pl.ds(target, 16)],
                send_sem=query_send.at[k],
                recv_sem=query_recv.at[k],
                device_id={"seq": peer},
                device_id_type=MESH,
            )
        )
        copies[-1].start()
    for copy in copies:
        copy.wait()
    put_trunk.wait()


def pair_kernel_body(
    n, block, keys, queries, weight, trunk_in, pair_out, trunk_out, keys3, qrows, qcols, sem
):
    step = pl.program_id(0)
    steps = pl.num_programs(0)
    width = keys.shape[0]
    pool_rows = width // n
    me = lax.axis_index("seq")

    @pl.when(step == 0)
    def _():
        pltpu.make_async_copy(trunk_in, trunk_out, sem).start()
        floats = keys[...].astype(F32)
        zero = jnp.zeros((1, 128), F32)
        keys3[:, 0:128] = jnp.concatenate([zero, floats[:-1]], axis=0).astype(BF16)
        keys3[:, 128:256] = keys[...]
        keys3[:, 256:384] = jnp.concatenate([floats[1:], zero], axis=0).astype(BF16)
        rows = queries[...].astype(F32)
        above = jnp.where(me > 0, rows[15:16], 0.0)
        below = jnp.where(me < n - 1, rows[16 + pool_rows : 17 + pool_rows], 0.0)
        rows = jnp.concatenate(
            [above, rows[16 : 16 + pool_rows], below, jnp.zeros((126 - pool_rows, 128), F32)],
            axis=0,
        )
        qrows[...] = rows[0 : qrows.shape[0]]
        cols = rows.T
        for i in range(pool_rows + 2):
            qcols[i] = jnp.broadcast_to(cols[:, i : i + 1], (128, 128)).astype(BF16)

    for half in range(block // 2):
        base = step * block + half * 2
        kernels = []
        for k in range(2):
            parts = []
            for b in range(3):
                parts.append(
                    qcols[base + k] * weight[0, b]
                    + qcols[base + k + 1] * weight[1, b]
                    + qcols[base + k + 2] * weight[2, b]
                )
            kernels.append(jnp.concatenate(parts, axis=0))
        conv = jnp.dot(
            keys3[...], jnp.concatenate(kernels, axis=1), preferred_element_type=F32
        ).astype(BF16)
        for k in range(2):
            row = jnp.broadcast_to(qrows[pl.ds(base + k + 1, 1), :], (16, 128)).astype(BF16)
            pair = (keys[...].reshape(width // 16, 16, 128) * row[None]).reshape(width, 128)
            pair_out[half * 2 + k] = pair + gelu(conv[:, k * 128 : k * 128 + 128])

    @pl.when(step == steps - 1)
    def _():
        pltpu.make_async_copy(trunk_in, trunk_out, sem).wait()


def on_device(
    n, bases, embed_table, norm_gains, depth_taps, point_weight, query_weight, key_weight, pair_kernel
):
    slab = bases.shape[0]
    channels = embed_table.shape[1]
    full = slab + 2 * HALO
    pool_rows = slab // POOL
    width = pool_rows * n
    hbm_spec = pl.BlockSpec(memory_space=pltpu.HBM)
    vmem_spec = pl.BlockSpec(memory_space=pltpu.VMEM)
    trunk, keys, queries = pl.pallas_call(
        functools.partial(trunk_kernel, n),
        out_shape=(
            jax.ShapeDtypeStruct((slab, channels), BF16),
            jax.ShapeDtypeStruct((width, 128), BF16),
            jax.ShapeDtypeStruct((pool_rows + 32, 128), BF16),
        ),
        in_specs=[hbm_spec] * 7,
        out_specs=(hbm_spec, vmem_spec, vmem_spec),
        scratch_shapes=[
            pltpu.VMEM((full, bases.shape[1]), jnp.int32),
            pltpu.VMEM(embed_table.shape, BF16),
            pltpu.VMEM(norm_gains.shape, F32),
            pltpu.VMEM((KW, 3, channels), F32),
            pltpu.VMEM(point_weight.shape, BF16),
            pltpu.VMEM(query_weight.shape, BF16),
            pltpu.VMEM(key_weight.shape, BF16),
            pltpu.VMEM((full, embed_table.shape[0]), BF16),
            pltpu.VMEM((full, channels), F32),
            pltpu.VMEM((2, full, channels), BF16),
            pltpu.VMEM((2, full, channels), BF16),
            pltpu.VMEM((slab, channels), BF16),
            pltpu.SemaphoreType.DMA((10,)),
            pltpu.SemaphoreType.DMA((2,)),
            pltpu.SemaphoreType.DMA((2,)),
            pltpu.SemaphoreType.DMA((2,)),
            pltpu.SemaphoreType.DMA((2,)),
            pltpu.SemaphoreType.DMA((n - 1,)),
            pltpu.SemaphoreType.DMA((n - 1,)),
        ],
        compiler_params=pltpu.CompilerParams(
            collective_id=0, has_side_effects=True, vmem_limit_bytes=63 * 1024 * 1024
        ),
        name="trunk_and_gather",
    )(bases, embed_table, norm_gains, depth_taps.swapaxes(0, 1), point_weight, query_weight, key_weight)

    block = 4
    pair_map, trunk = pl.pallas_call(
        functools.partial(pair_kernel_body, n, block),
        grid=(pool_rows // block,),
        out_shape=(
            jax.ShapeDtypeStruct((pool_rows, width, 128), BF16),
            jax.ShapeDtypeStruct((slab, channels), BF16),
        ),
        in_specs=[
            pl.BlockSpec((width, 128), lambda i: (0, 0)),
            pl.BlockSpec((pool_rows + 32, 128), lambda i: (0, 0)),
            pl.BlockSpec((3, 3, 128, 128), lambda i: (0, 0, 0, 0)),
            hbm_spec,
        ],
        out_specs=(pl.BlockSpec((block, width, 128), lambda i: (i, 0, 0)), hbm_spec),
        scratch_shapes=[
            pltpu.VMEM((width, 384), BF16),
            pltpu.VMEM((pool_rows + 8, 128), F32),
            pltpu.VMEM((pool_rows + 2, 128, 128), BF16),
            pltpu.SemaphoreType.DMA,
        ],
        compiler_params=pltpu.CompilerParams(vmem_limit_bytes=63 * 1024 * 1024),
        name="pair_map",
    )(keys, queries, pair_kernel, trunk)
    return (trunk, pair_map)


def solution(mesh):
    return jax.shard_map(
        functools.partial(on_device, mesh.shape["seq"]),
        mesh=mesh,
        in_specs=(P(("batch", "seq"), None), P(), P(), P(), P(), P(), P(), P()),
        out_specs=(P(("batch", "seq"), None), P(("batch", "seq"), None, None)),
        check_vma=False,
    )
```

```python
import functools

import jax
import jax.numpy as jnp
from jax import lax
from jax.experimental import pallas as pl
from jax.experimental.pallas import tpu as pltpu
from jax.sharding import PartitionSpec as P

KW = 5
DILATIONS = (2, 8, 32)
POOL = 16
HALO = 96
CHUNK = 32
GELU_A = 0.7978845608028654
GELU_B = 0.7978845608028654 * 0.044715
MESH = pl.DeviceIdType.MESH
F32 = jnp.float32
BF16 = jnp.bfloat16


def gelu(v):
    half = 0.5 * v
    return half + half * jnp.tanh(v * (GELU_A + GELU_B * (v * v)))


def blocks_of(rows):
    units = rows // 16
    sizes = [(units + 2 - k) // 3 * 16 for k in range(3)]
    return [(sum(sizes[:k]), sizes[k]) for k in range(3)]


def pieces_of(low, rows, most):
    return [(low + at, min(most, rows - at)) for at in range(0, rows, most)]


def interleave(first, second):
    count = max(len(first), len(second), 1)
    done = [0, 0]
    for k in range(count):
        for which, tasks in enumerate((first, second)):
            target = len(tasks) * (k + 1) // count
            while done[which] < target:
                tasks[done[which]]()
                done[which] += 1


def trunk_kernel(
    n,
    bases,
    table,
    gains,
    taps,
    point,
    query_w,
    key_w,
    trunk_out,
    keys,
    queries,
    base_v,
    table_v,
    gains_v,
    taps_v,
    point_v,
    qw_v,
    kw_v,
    hot,
    xs,
    nrm,
    act,
    trunk_v,
    local_sem,
    halo_send,
    halo_recv,
    query_send,
    query_recv,
    send_sem,
    recv_sem,
):
    slab = bases.shape[0]
    channels = table.shape[1]
    full = slab + 2 * HALO
    pool_rows = slab // POOL
    me = lax.axis_index("seq")
    right = lax.rem(me + 1, n)
    left = lax.rem(me + n - 1, n)

    barrier = pltpu.get_barrier_semaphore()
    for d in range(1, n):
        pl.semaphore_signal(
            barrier, inc=1, device_id={"seq": lax.rem(me + d, n)}, device_id_type=MESH
        )

    def fetch(source, target, k):
        copy = pltpu.make_async_copy(source, target, local_sem.at[k])
        copy.start()
        return copy

    own = fetch(bases, base_v.at[pl.ds(HALO, slab)], 0)
    get_table = fetch(table, table_v, 1)
    weights = [fetch(gains, gains_v, 2), fetch(taps, taps_v, 3)]
    for layer in range(3):
        weights.append(fetch(point.at[layer], point_v.at[layer], 4 + layer))
    weights.append(fetch(query_w, qw_v, 7))
    weights.append(fetch(key_w, kw_v, 8))

    width = table.shape[0]
    places = width // 4
    spread = (
        lax.broadcasted_iota(jnp.int32, (places, width), 1) // 4
        == lax.broadcasted_iota(jnp.int32, (places, width), 0)
    ).astype(BF16)
    letter = (lax.broadcasted_iota(jnp.int32, (1, width), 1) % 4).astype(F32)

    def one_hot(start, rows):
        codes = base_v[pl.ds(start, rows), :].astype(F32).astype(BF16)
        wide = jnp.dot(codes, spread, preferred_element_type=F32)
        hot[pl.ds(start, rows), :] = jnp.where(wide == letter, 1.0, 0.0).astype(BF16)

    def embed(start, rows):
        for col in range(0, channels, 256):
            xs[pl.ds(start, rows), pl.ds(col, 256)] = jnp.dot(
                hot[pl.ds(start, rows), :],
                table_v[:, pl.ds(col, 256)],
                preferred_element_type=F32,
            )

    own.wait()
    one_hot(HALO, slab)
    pl.semaphore_wait(barrier, n - 1)
    to_right = pltpu.make_async_remote_copy(
        src_ref=bases.at[pl.ds(slab - HALO, HALO)],
        dst_ref=base_v.at[pl.ds(0, HALO)],
        send_sem=halo_send.at[0],
        recv_sem=halo_recv.at[0],
        device_id={"seq": right},
        device_id_type=MESH,
    )
    to_right.start()
    to_left = pltpu.make_async_remote_copy(
        src_ref=bases.at[pl.ds(0, HALO)],
        dst_ref=base_v.at[pl.ds(HALO + slab, HALO)],
        send_sem=halo_send.at[1],
        recv_sem=halo_recv.at[1],
        device_id={"seq": left},
        device_id_type=MESH,
    )
    to_left.start()

    first_row = me * slab - HALO
    last_row = n * slab
    reaches = [2 * s for s in DILATIONS]
    lows = [HALO - sum(reaches[layer + 1 :]) for layer in range(3)]
    scaled = []

    def norm_piece(layer, r, rows):
        floats = xs[pl.ds(r, rows), :]
        mean = jnp.sum(floats * floats, axis=1, keepdims=True) * (1.0 / channels)
        scale = lax.rsqrt(mean + 1e-6)
        if r < HALO or r + rows > HALO + slab:
            place = first_row + r + lax.broadcasted_iota(jnp.int32, (rows, 1), 0)
            inside = jnp.logical_and(place >= 0, place < last_row)
            scale = jnp.where(inside, scale, 0.0)
        nrm[layer % 2, pl.ds(r, rows), :] = (floats * scale).astype(BF16)

    def norms(layer, low, rows):
        return [
            functools.partial(norm_piece, layer, r, size) for r, size in pieces_of(low, rows, 32)
        ]

    def conv_piece(layer, r, rows, col):
        s = DILATIONS[layer]
        total = None
        low = (r - 2 * s) // 16 * 16
        span = -(-(r + rows + 2 * s - low) // 16) * 16
        if s % 16:
            near = nrm[layer % 2, pl.ds(low, span), pl.ds(col, 128)]
        for t in range(KW):
            at = r + (t - 2) * s
            if s % 16:
                part = near[at - low : at - low + rows]
            else:
                part = nrm[layer % 2, pl.ds(at, rows), pl.ds(col, 128)]
            term = part * scaled[layer][t : t + 1, col : col + 128]
            total = term if total is None else total + term
        act[layer % 2, pl.ds(r, rows), pl.ds(col, 128)] = gelu(total)

    def convs(layer, k):
        at, size = blocks_of(full - 2 * lows[layer])[k]
        return [
            functools.partial(conv_piece, layer, r, rows, col)
            for r, rows in pieces_of(lows[layer] + at, size, 32)
            for col in range(0, channels, 128)
        ]

    def mix_piece(layer, r, rows, col):
        mixed = xs[pl.ds(r, rows), pl.ds(col, 256)] + jnp.dot(
            act[layer % 2, pl.ds(r, rows), :],
            point_v[layer, :, pl.ds(col, 256)],
            preferred_element_type=F32,
        )
        if layer < 2:
            xs[pl.ds(r, rows), pl.ds(col, 256)] = mixed
        else:
            trunk_v[pl.ds(r - HALO, rows), pl.ds(col, 256)] = mixed.astype(BF16)

    def mixes(layer, k):
        at, size = blocks_of(full - 2 * lows[layer])[k]
        return [
            functools.partial(mix_piece, layer, lows[layer] + at, size, col)
            for col in range(0, channels, 256)
        ]

    def next_norms(layer, k):
        if layer == 2:
            return []
        at, size = blocks_of(full - 2 * lows[layer])[k]
        return norms(layer + 1, lows[layer] + at, size)

    get_table.wait()
    for at in range(0, slab, slab // 2):
        embed(HALO + at, slab // 2)
    for task in norms(0, HALO, slab):
        task()
    to_right.wait()
    to_left.wait()
    for start in (0, HALO + slab):
        one_hot(start, HALO)
        embed(start, HALO)
    for weight in weights:
        weight.wait()
    for layer in range(3):
        scaled.append((taps_v[:, layer] * gains_v[pl.ds(layer, 1), :]).astype(BF16))
    for task in norms(0, 0, HALO) + norms(0, HALO + slab, HALO):
        task()

    interleave(convs(0, 0), [])
    for layer in range(3):
        interleave(mixes(layer, 0), convs(layer, 1))
        interleave(mixes(layer, 1), next_norms(layer, 0) + convs(layer, 2))
        following = convs(layer + 1, 0) if layer < 2 else []
        interleave(mixes(layer, 2), next_norms(layer, 1) + following)
        interleave([], next_norms(layer, 2))

    put_trunk = pltpu.make_async_copy(trunk_v, trunk_out, local_sem.at[9])
    put_trunk.start()
    group = lax.broadcasted_iota(jnp.int32, (pool_rows, slab), 1) // POOL
    pooler = jnp.where(
        group == lax.broadcasted_iota(jnp.int32, (pool_rows, slab), 0), 1.0 / POOL, 0.0
    ).astype(BF16)
    pooled = jnp.dot(pooler, trunk_v[...], preferred_element_type=F32).astype(BF16)
    mine = pl.ds(pl.multiple_of(me * pool_rows, pool_rows), pool_rows)
    keys[mine, :] = jnp.dot(pooled, kw_v[...], preferred_element_type=F32).astype(BF16)

    copies = []
    for d in sorted(range(1, n), key=lambda d: -min(d, n - d)):
        copies.append(
            pltpu.make_async_remote_copy(
                src_ref=keys.at[mine],
                dst_ref=keys.at[mine],
                send_sem=send_sem.at[d - 1],
                recv_sem=recv_sem.at[d - 1],
                device_id={"seq": lax.rem(me + d, n)},
                device_id_type=MESH,
            )
        )
        copies[-1].start()
    queries[pl.ds(16, pool_rows), :] = jnp.dot(
        pooled, qw_v[...], preferred_element_type=F32
    ).astype(BF16)
    for k, (source, target, peer) in enumerate(
        ((pool_rows, 0, right), (16, 16 + pool_rows, left))
    ):
        copies.append(
            pltpu.make_async_remote_copy(
                src_ref=queries.at[pl.ds(source, 16)],
                dst_ref=queries.at[pl.ds(target, 16)],
                send_sem=query_send.at[k],
                recv_sem=query_recv.at[k],
                device_id={"seq": peer},
                device_id_type=MESH,
            )
        )
        copies[-1].start()
    for copy in copies:
        copy.wait()
    put_trunk.wait()


def pair_kernel_body(
    n, block, keys, queries, weight, trunk_in, pair_out, trunk_out, keys3, qrows, qcols, trunk_v, sem
):
    step = pl.program_id(0)
    steps = pl.num_programs(0)
    width = keys.shape[0]
    pool_rows = width // n
    me = lax.axis_index("seq")

    @pl.when(step == 0)
    def _():
        pltpu.make_async_copy(trunk_in, trunk_v, sem.at[0]).start()
        floats = keys[...].astype(F32)
        zero = jnp.zeros((1, 128), F32)
        keys3[:, 0:128] = jnp.concatenate([zero, floats[:-1]], axis=0).astype(BF16)
        keys3[:, 128:256] = keys[...]
        keys3[:, 256:384] = jnp.concatenate([floats[1:], zero], axis=0).astype(BF16)
        rows = queries[...].astype(F32)
        above = jnp.where(me > 0, rows[15:16], 0.0)
        below = jnp.where(me < n - 1, rows[16 + pool_rows : 17 + pool_rows], 0.0)
        rows = jnp.concatenate(
            [above, rows[16 : 16 + pool_rows], below, jnp.zeros((126 - pool_rows, 128), F32)],
            axis=0,
        )
        qrows[...] = rows[0 : qrows.shape[0]]
        cols = rows.T
        for i in range(pool_rows + 2):
            qcols[i] = jnp.broadcast_to(cols[:, i : i + 1], (128, 128)).astype(BF16)

    for half in range(block // 2):
        base = step * block + half * 2
        kernels = []
        for k in range(2):
            parts = []
            for b in range(3):
                parts.append(
                    qcols[base + k] * weight[0, b]
                    + qcols[base + k + 1] * weight[1, b]
                    + qcols[base + k + 2] * weight[2, b]
                )
            kernels.append(jnp.concatenate(parts, axis=0))
        conv = jnp.dot(
            keys3[...], jnp.concatenate(kernels, axis=1), preferred_element_type=F32
        ).astype(BF16)
        for k in range(2):
            row = jnp.broadcast_to(qrows[pl.ds(base + k + 1, 1), :], (16, 128)).astype(BF16)
            pair = (keys[...].reshape(width // 16, 16, 128) * row[None]).reshape(width, 128)
            pair_out[half * 2 + k] = pair + gelu(conv[:, k * 128 : k * 128 + 128])

    @pl.when(step == 0)
    def _():
        pltpu.make_async_copy(trunk_in, trunk_v, sem.at[0]).wait()
        pltpu.make_async_copy(trunk_v, trunk_out, sem.at[1]).start()

    @pl.when(step == steps - 1)
    def _():
        pltpu.make_async_copy(trunk_v, trunk_out, sem.at[1]).wait()


def on_device(
    n, bases, embed_table, norm_gains, depth_taps, point_weight, query_weight, key_weight, pair_kernel
):
    slab = bases.shape[0]
    channels = embed_table.shape[1]
    full = slab + 2 * HALO
    pool_rows = slab // POOL
    width = pool_rows * n
    hbm_spec = pl.BlockSpec(memory_space=pltpu.HBM)
    vmem_spec = pl.BlockSpec(memory_space=pltpu.VMEM)
    trunk, keys, queries = pl.pallas_call(
        functools.partial(trunk_kernel, n),
        out_shape=(
            jax.ShapeDtypeStruct((slab, channels), BF16),
            jax.ShapeDtypeStruct((width, 128), BF16),
            jax.ShapeDtypeStruct((pool_rows + 32, 128), BF16),
        ),
        in_specs=[hbm_spec] * 7,
        out_specs=(hbm_spec, vmem_spec, vmem_spec),
        scratch_shapes=[
            pltpu.VMEM((full, bases.shape[1]), jnp.int32),
            pltpu.VMEM(embed_table.shape, BF16),
            pltpu.VMEM(norm_gains.shape, F32),
            pltpu.VMEM((KW, 3, channels), F32),
            pltpu.VMEM(point_weight.shape, BF16),
            pltpu.VMEM(query_weight.shape, BF16),
            pltpu.VMEM(key_weight.shape, BF16),
            pltpu.VMEM((full, embed_table.shape[0]), BF16),
            pltpu.VMEM((full, channels), F32),
            pltpu.VMEM((2, full, channels), BF16),
            pltpu.VMEM((2, full, channels), BF16),
            pltpu.VMEM((slab, channels), BF16),
            pltpu.SemaphoreType.DMA((10,)),
            pltpu.SemaphoreType.DMA((2,)),
            pltpu.SemaphoreType.DMA((2,)),
            pltpu.SemaphoreType.DMA((2,)),
            pltpu.SemaphoreType.DMA((2,)),
            pltpu.SemaphoreType.DMA((n - 1,)),
            pltpu.SemaphoreType.DMA((n - 1,)),
        ],
        compiler_params=pltpu.CompilerParams(
            collective_id=0, has_side_effects=True, vmem_limit_bytes=63 * 1024 * 1024
        ),
        name="trunk_and_gather",
    )(bases, embed_table, norm_gains, depth_taps.swapaxes(0, 1), point_weight, query_weight, key_weight)

    block = 4
    pair_map, trunk = pl.pallas_call(
        functools.partial(pair_kernel_body, n, block),
        grid=(pool_rows // block,),
        out_shape=(
            jax.ShapeDtypeStruct((pool_rows, width, 128), BF16),
            jax.ShapeDtypeStruct((slab, channels), BF16),
        ),
        in_specs=[
            pl.BlockSpec((width, 128), lambda i: (0, 0)),
            pl.BlockSpec((pool_rows + 32, 128), lambda i: (0, 0)),
            pl.BlockSpec((3, 3, 128, 128), lambda i: (0, 0, 0, 0)),
            hbm_spec,
        ],
        out_specs=(pl.BlockSpec((block, width, 128), lambda i: (i, 0, 0)), hbm_spec),
        scratch_shapes=[
            pltpu.VMEM((width, 384), BF16),
            pltpu.VMEM((pool_rows + 8, 128), F32),
            pltpu.VMEM((pool_rows + 2, 128, 128), BF16),
            pltpu.VMEM((slab, channels), BF16),
            pltpu.SemaphoreType.DMA((2,)),
        ],
        compiler_params=pltpu.CompilerParams(vmem_limit_bytes=63 * 1024 * 1024),
        name="pair_map",
    )(keys, queries, pair_kernel, trunk)
    return (trunk, pair_map)


def solution(mesh):
    return jax.shard_map(
        functools.partial(on_device, mesh.shape["seq"]),
        mesh=mesh,
        in_specs=(P(("batch", "seq"), None), P(), P(), P(), P(), P(), P(), P()),
        out_specs=(P(("batch", "seq"), None), P(("batch", "seq"), None, None)),
        check_vma=False,
    )
```

```python
import functools

import jax
import jax.numpy as jnp
from jax import lax
from jax.experimental import pallas as pl
from jax.experimental.pallas import tpu as pltpu
from jax.sharding import PartitionSpec as P

KW = 5
DILATIONS = (2, 8, 32)
POOL = 16
HALO = 96
CHUNK = 32
GELU_A = 0.7978845608028654
GELU_B = 0.7978845608028654 * 0.044715
MESH = pl.DeviceIdType.MESH
F32 = jnp.float32
BF16 = jnp.bfloat16


def gelu(v):
    half = 0.5 * v
    return half + half * jnp.tanh(v * (GELU_A + GELU_B * (v * v)))


def blocks_of(rows):
    units = rows // 16
    sizes = [(units + 2 - k) // 3 * 16 for k in range(3)]
    return [(sum(sizes[:k]), sizes[k]) for k in range(3)]


def pieces_of(low, rows, most):
    return [(low + at, min(most, rows - at)) for at in range(0, rows, most)]


def interleave(first, second):
    count = max(len(first), len(second), 1)
    done = [0, 0]
    for k in range(count):
        for which, tasks in enumerate((first, second)):
            target = len(tasks) * (k + 1) // count
            while done[which] < target:
                tasks[done[which]]()
                done[which] += 1


def trunk_kernel(
    n,
    bases,
    table,
    gains,
    taps,
    point,
    query_w,
    key_w,
    weight,
    trunk_out,
    keys,
    queries,
    weff,
    base_v,
    table_v,
    gains_v,
    taps_v,
    point_v,
    qw_v,
    kw_v,
    weight_v,
    qcols,
    hot,
    xs,
    nrm,
    act,
    trunk_v,
    local_sem,
    halo_send,
    halo_recv,
    query_send,
    query_recv,
    send_sem,
    recv_sem,
):
    slab = bases.shape[0]
    channels = table.shape[1]
    full = slab + 2 * HALO
    pool_rows = slab // POOL
    me = lax.axis_index("seq")
    right = lax.rem(me + 1, n)
    left = lax.rem(me + n - 1, n)

    barrier = pltpu.get_barrier_semaphore()
    for d in range(1, n):
        pl.semaphore_signal(
            barrier, inc=1, device_id={"seq": lax.rem(me + d, n)}, device_id_type=MESH
        )

    def fetch(source, target, k):
        copy = pltpu.make_async_copy(source, target, local_sem.at[k])
        copy.start()
        return copy

    own = fetch(bases, base_v.at[pl.ds(HALO, slab)], 0)
    get_table = fetch(table, table_v, 1)
    weights = [fetch(gains, gains_v, 2), fetch(taps, taps_v, 3)]
    for layer in range(3):
        weights.append(fetch(point.at[layer], point_v.at[layer], 4 + layer))
    weights.append(fetch(query_w, qw_v, 7))
    weights.append(fetch(key_w, kw_v, 8))
    weights.append(fetch(weight, weight_v, 10))

    width = table.shape[0]
    places = width // 4
    spread = (
        lax.broadcasted_iota(jnp.int32, (places, width), 1) // 4
        == lax.broadcasted_iota(jnp.int32, (places, width), 0)
    ).astype(BF16)
    letter = (lax.broadcasted_iota(jnp.int32, (1, width), 1) % 4).astype(F32)

    def one_hot(start, rows):
        codes = base_v[pl.ds(start, rows), :].astype(F32).astype(BF16)
        wide = jnp.dot(codes, spread, preferred_element_type=F32)
        hot[pl.ds(start, rows), :] = jnp.where(wide == letter, 1.0, 0.0).astype(BF16)

    def embed(start, rows):
        for col in range(0, channels, 256):
            xs[pl.ds(start, rows), pl.ds(col, 256)] = jnp.dot(
                hot[pl.ds(start, rows), :],
                table_v[:, pl.ds(col, 256)],
                preferred_element_type=F32,
            )

    own.wait()
    one_hot(HALO, slab)
    pl.semaphore_wait(barrier, n - 1)
    to_right = pltpu.make_async_remote_copy(
        src_ref=bases.at[pl.ds(slab - HALO, HALO)],
        dst_ref=base_v.at[pl.ds(0, HALO)],
        send_sem=halo_send.at[0],
        recv_sem=halo_recv.at[0],
        device_id={"seq": right},
        device_id_type=MESH,
    )
    to_right.start()
    to_left = pltpu.make_async_remote_copy(
        src_ref=bases.at[pl.ds(0, HALO)],
        dst_ref=base_v.at[pl.ds(HALO + slab, HALO)],
        send_sem=halo_send.at[1],
        recv_sem=halo_recv.at[1],
        device_id={"seq": left},
        device_id_type=MESH,
    )
    to_left.start()

    first_row = me * slab - HALO
    last_row = n * slab
    reaches = [2 * s for s in DILATIONS]
    lows = [HALO - sum(reaches[layer + 1 :]) for layer in range(3)]
    scaled = []

    def norm_piece(layer, r, rows):
        floats = xs[pl.ds(r, rows), :]
        mean = jnp.sum(floats * floats, axis=1, keepdims=True) * (1.0 / channels)
        scale = lax.rsqrt(mean + 1e-6)
        if r < HALO or r + rows > HALO + slab:
            place = first_row + r + lax.broadcasted_iota(jnp.int32, (rows, 1), 0)
            inside = jnp.logical_and(place >= 0, place < last_row)
            scale = jnp.where(inside, scale, 0.0)
        nrm[layer % 2, pl.ds(r, rows), :] = (floats * scale).astype(BF16)

    def norms(layer, low, rows):
        return [
            functools.partial(norm_piece, layer, r, size) for r, size in pieces_of(low, rows, 32)
        ]

    def conv_piece(layer, r, rows, col):
        s = DILATIONS[layer]
        total = None
        low = (r - 2 * s) // 16 * 16
        span = -(-(r + rows + 2 * s - low) // 16) * 16
        if s % 16:
            near = nrm[layer % 2, pl.ds(low, span), pl.ds(col, 128)]
        for t in range(KW):
            at = r + (t - 2) * s
            if s % 16:
                part = near[at - low : at - low + rows]
            else:
                part = nrm[layer % 2, pl.ds(at, rows), pl.ds(col, 128)]
            term = part * scaled[layer][t : t + 1, col : col + 128]
            total = term if total is None else total + term
        act[layer % 2, pl.ds(r, rows), pl.ds(col, 128)] = gelu(total)

    def convs(layer, k):
        at, size = blocks_of(full - 2 * lows[layer])[k]
        return [
            functools.partial(conv_piece, layer, r, rows, col)
            for r, rows in pieces_of(lows[layer] + at, size, 112)
            for col in range(0, channels, 128)
        ]

    def mix_piece(layer, r, rows, col):
        mixed = xs[pl.ds(r, rows), pl.ds(col, 256)] + jnp.dot(
            act[layer % 2, pl.ds(r, rows), :],
            point_v[layer, :, pl.ds(col, 256)],
            preferred_element_type=F32,
        )
        if layer < 2:
            xs[pl.ds(r, rows), pl.ds(col, 256)] = mixed
        else:
            trunk_v[pl.ds(r - HALO, rows), pl.ds(col, 256)] = mixed.astype(BF16)

    def mixes(layer, k):
        at, size = blocks_of(full - 2 * lows[layer])[k]
        return [
            functools.partial(mix_piece, layer, lows[layer] + at, size, col)
            for col in range(0, channels, 256)
        ]

    def next_norms(layer, k):
        if layer == 2:
            return []
        at, size = blocks_of(full - 2 * lows[layer])[k]
        return norms(layer + 1, lows[layer] + at, size)

    get_table.wait()
    for at in range(0, slab, slab // 2):
        embed(HALO + at, slab // 2)
    for task in norms(0, HALO, slab):
        task()
    to_right.wait()
    to_left.wait()
    for start in (0, HALO + slab):
        one_hot(start, HALO)
        embed(start, HALO)
    for weight in weights:
        weight.wait()
    for layer in range(3):
        scaled.append((taps_v[:, layer] * gains_v[pl.ds(layer, 1), :]).astype(BF16))
    for task in norms(0, 0, HALO) + norms(0, HALO + slab, HALO):
        task()

    interleave(convs(0, 0), [])
    for layer in range(3):
        interleave(mixes(layer, 0), convs(layer, 1))
        interleave(mixes(layer, 1), next_norms(layer, 0) + convs(layer, 2))
        following = convs(layer + 1, 0) if layer < 2 else []
        interleave(mixes(layer, 2), next_norms(layer, 1) + following)
        interleave([], next_norms(layer, 2))

    put_trunk = pltpu.make_async_copy(trunk_v, trunk_out, local_sem.at[9])
    put_trunk.start()
    group = lax.broadcasted_iota(jnp.int32, (pool_rows, slab), 1) // POOL
    pooler = jnp.where(
        group == lax.broadcasted_iota(jnp.int32, (pool_rows, slab), 0), 1.0 / POOL, 0.0
    ).astype(BF16)
    pooled = jnp.dot(pooler, trunk_v[...], preferred_element_type=F32).astype(BF16)
    mine = pl.ds(pl.multiple_of(me * pool_rows, pool_rows), pool_rows)
    keys[mine, :] = jnp.dot(pooled, kw_v[...], preferred_element_type=F32).astype(BF16)

    copies = []
    for d in sorted(range(1, n), key=lambda d: -min(d, n - d)):
        copies.append(
            pltpu.make_async_remote_copy(
                src_ref=keys.at[mine],
                dst_ref=keys.at[mine],
                send_sem=send_sem.at[d - 1],
                recv_sem=recv_sem.at[d - 1],
                device_id={"seq": lax.rem(me + d, n)},
                device_id_type=MESH,
            )
        )
        copies[-1].start()
    own_queries = jnp.dot(pooled, qw_v[...], preferred_element_type=F32).astype(BF16)
    queries[pl.ds(16, pool_rows), :] = own_queries
    for k, (source, target, peer) in enumerate(
        ((pool_rows, 0, right), (16, 16 + pool_rows, left))
    ):
        copies.append(
            pltpu.make_async_remote_copy(
                src_ref=queries.at[pl.ds(source, 16)],
                dst_ref=queries.at[pl.ds(target, 16)],
                send_sem=query_send.at[k],
                recv_sem=query_recv.at[k],
                device_id={"seq": peer},
                device_id_type=MESH,
            )
        )
        copies[-1].start()

    def spread_rows(rows, places):
        short = 128 - rows.shape[0]
        cols = jnp.concatenate([rows, jnp.zeros((short, 128), F32)], axis=0).T
        for source, target in places:
            qcols[target] = jnp.broadcast_to(cols[:, source : source + 1], (128, 128)).astype(BF16)

    def combine(i):
        for b in range(3):
            weff[i // 2, pl.ds(b * 128, 128), pl.ds(i % 2 * 128, 128)] = (
                qcols[i] * weight_v[0, b]
                + qcols[i + 1] * weight_v[1, b]
                + qcols[i + 2] * weight_v[2, b]
            )

    spread_rows(own_queries.astype(F32), [(i, i + 1) for i in range(pool_rows)])
    for i in range(1, pool_rows - 1):
        combine(i)
    for copy in copies[-2:]:
        copy.wait()
    above = jnp.where(me > 0, queries[0:16, :].astype(F32), 0.0)
    below = jnp.where(me < n - 1, queries[pl.ds(16 + pool_rows, 16), :].astype(F32), 0.0)
    spread_rows(jnp.concatenate([above, below], axis=0), [(15, 0), (16, pool_rows + 1)])
    combine(0)
    combine(pool_rows - 1)
    for copy in copies[:-2]:
        copy.wait()
    put_trunk.wait()


def pair_kernel_body(
    n, block, keys, queries, weff, trunk_in, pair_out, trunk_out, keys3, qrows, trunk_v, sem
):
    step = pl.program_id(0)
    steps = pl.num_programs(0)
    width = keys.shape[0]
    pool_rows = width // n

    @pl.when(step == 0)
    def _():
        pltpu.make_async_copy(trunk_in, trunk_v, sem.at[0]).start()
        floats = keys[...].astype(F32)
        zero = jnp.zeros((1, 128), F32)
        keys3[:, 0:128] = jnp.concatenate([zero, floats[:-1]], axis=0).astype(BF16)
        keys3[:, 128:256] = keys[...]
        keys3[:, 256:384] = jnp.concatenate([floats[1:], zero], axis=0).astype(BF16)
        qrows[...] = queries[pl.ds(16, pool_rows), :].astype(F32)

    for half in range(block // 2):
        base = step * block + half * 2
        conv = jnp.dot(keys3[...], weff[half], preferred_element_type=F32).astype(BF16)
        for k in range(2):
            row = jnp.broadcast_to(qrows[pl.ds(base + k, 1), :], (16, 128)).astype(BF16)
            pair = (keys[...].reshape(width // 16, 16, 128) * row[None]).reshape(width, 128)
            pair_out[half * 2 + k] = pair + gelu(conv[:, k * 128 : k * 128 + 128])

    @pl.when(step == 0)
    def _():
        pltpu.make_async_copy(trunk_in, trunk_v, sem.at[0]).wait()
        pltpu.make_async_copy(trunk_v, trunk_out, sem.at[1]).start()

    @pl.when(step == steps - 1)
    def _():
        pltpu.make_async_copy(trunk_v, trunk_out, sem.at[1]).wait()


def on_device(
    n, bases, embed_table, norm_gains, depth_taps, point_weight, query_weight, key_weight, pair_kernel
):
    slab = bases.shape[0]
    channels = embed_table.shape[1]
    full = slab + 2 * HALO
    pool_rows = slab // POOL
    width = pool_rows * n
    hbm_spec = pl.BlockSpec(memory_space=pltpu.HBM)
    vmem_spec = pl.BlockSpec(memory_space=pltpu.VMEM)
    trunk, keys, queries, weff = pl.pallas_call(
        functools.partial(trunk_kernel, n),
        out_shape=(
            jax.ShapeDtypeStruct((slab, channels), BF16),
            jax.ShapeDtypeStruct((width, 128), BF16),
            jax.ShapeDtypeStruct((pool_rows + 32, 128), BF16),
            jax.ShapeDtypeStruct((pool_rows // 2, 384, 256), BF16),
        ),
        in_specs=[hbm_spec] * 8,
        out_specs=(hbm_spec, vmem_spec, vmem_spec, vmem_spec),
        scratch_shapes=[
            pltpu.VMEM((full, bases.shape[1]), jnp.int32),
            pltpu.VMEM(embed_table.shape, BF16),
            pltpu.VMEM(norm_gains.shape, F32),
            pltpu.VMEM((KW, 3, channels), F32),
            pltpu.VMEM(point_weight.shape, BF16),
            pltpu.VMEM(query_weight.shape, BF16),
            pltpu.VMEM(key_weight.shape, BF16),
            pltpu.VMEM(pair_kernel.shape, BF16),
            pltpu.VMEM((pool_rows + 2, 128, 128), BF16),
            pltpu.VMEM((full, embed_table.shape[0]), BF16),
            pltpu.VMEM((full, channels), F32),
            pltpu.VMEM((2, full, channels), BF16),
            pltpu.VMEM((2, full, channels), BF16),
            pltpu.VMEM((slab, channels), BF16),
            pltpu.SemaphoreType.DMA((11,)),
            pltpu.SemaphoreType.DMA((2,)),
            pltpu.SemaphoreType.DMA((2,)),
            pltpu.SemaphoreType.DMA((2,)),
            pltpu.SemaphoreType.DMA((2,)),
            pltpu.SemaphoreType.DMA((n - 1,)),
            pltpu.SemaphoreType.DMA((n - 1,)),
        ],
        compiler_params=pltpu.CompilerParams(
            collective_id=0, has_side_effects=True, vmem_limit_bytes=32 * 1024 * 1024
        ),
        name="trunk_and_gather",
    )(
        *(
            pltpu.with_memory_space_constraint(array, pltpu.HBM)
            for array in (
                bases,
                embed_table,
                norm_gains,
                depth_taps.swapaxes(0, 1),
                point_weight,
                query_weight,
                key_weight,
                pair_kernel,
            )
        )
    )

    block = 8
    pair_map, trunk = pl.pallas_call(
        functools.partial(pair_kernel_body, n, block),
        grid=(pool_rows // block,),
        out_shape=(
            jax.ShapeDtypeStruct((pool_rows, width, 128), BF16),
            jax.ShapeDtypeStruct((slab, channels), BF16),
        ),
        in_specs=[
            pl.BlockSpec((width, 128), lambda i: (0, 0)),
            pl.BlockSpec((pool_rows + 32, 128), lambda i: (0, 0)),
            pl.BlockSpec((block // 2, 384, 256), lambda i: (i, 0, 0)),
            hbm_spec,
        ],
        out_specs=(pl.BlockSpec((block, width, 128), lambda i: (i, 0, 0)), hbm_spec),
        scratch_shapes=[
            pltpu.VMEM((width, 384), BF16),
            pltpu.VMEM((pool_rows, 128), F32),
            pltpu.VMEM((slab, channels), BF16),
            pltpu.SemaphoreType.DMA((2,)),
        ],
        compiler_params=pltpu.CompilerParams(vmem_limit_bytes=32 * 1024 * 1024),
        name="pair_map",
    )(keys, queries, weff, trunk)
    return (trunk, pair_map)


def solution(mesh):
    return jax.shard_map(
        functools.partial(on_device, mesh.shape["seq"]),
        mesh=mesh,
        in_specs=(P(("batch", "seq"), None), P(), P(), P(), P(), P(), P(), P()),
        out_specs=(P(("batch", "seq"), None), P(("batch", "seq"), None, None)),
        check_vma=False,
    )
```

```python
import functools

import jax
import jax.numpy as jnp
from jax import lax
from jax.experimental import pallas as pl
from jax.experimental.pallas import tpu as pltpu
from jax.sharding import PartitionSpec as P

KW = 5
DILATIONS = (2, 8, 32)
POOL = 16
HALO = 96
CHUNK = 32
GELU_A = 0.7978845608028654
GELU_B = 0.7978845608028654 * 0.044715
MESH = pl.DeviceIdType.MESH
F32 = jnp.float32
BF16 = jnp.bfloat16


def gelu_of_half(half):
    return half + half * jnp.tanh(half * (2 * GELU_A + 8 * GELU_B * (half * half)))


def pieces_of(low, rows, most):
    return [(low + at, min(most, rows - at)) for at in range(0, rows, most)]


def interleave(first, second):
    count = max(len(first), len(second), 1)
    done = [0, 0]
    for k in range(count):
        for which, tasks in enumerate((first, second)):
            target = len(tasks) * (k + 1) // count
            while done[which] < target:
                tasks[done[which]]()
                done[which] += 1


def trunk_kernel(
    n,
    bases,
    table,
    gains,
    taps,
    point,
    query_w,
    key_w,
    weight,
    trunk_out,
    keys,
    queries,
    weff,
    base_v,
    table_v,
    gains_v,
    taps_v,
    point_v,
    qw_v,
    kw_v,
    weight_v,
    qcols,
    hot,
    xs,
    nrm,
    act,
    trunk_v,
    local_sem,
    halo_send,
    halo_recv,
    query_send,
    query_recv,
    send_sem,
    recv_sem,
):
    slab = bases.shape[0]
    channels = table.shape[1]
    full = slab + 2 * HALO
    pool_rows = slab // POOL
    me = lax.axis_index("seq")
    right = lax.rem(me + 1, n)
    left = lax.rem(me + n - 1, n)

    barrier = pltpu.get_barrier_semaphore()
    for d in range(1, n):
        pl.semaphore_signal(
            barrier, inc=1, device_id={"seq": lax.rem(me + d, n)}, device_id_type=MESH
        )

    def fetch(source, target, k):
        copy = pltpu.make_async_copy(source, target, local_sem.at[k])
        copy.start()
        return copy

    own = fetch(bases, base_v.at[pl.ds(HALO, slab)], 0)
    get_table = fetch(table, table_v, 1)
    weights = [fetch(gains, gains_v, 2), fetch(taps, taps_v, 3)]
    for layer in range(3):
        weights.append(fetch(point.at[layer], point_v.at[layer], 4 + layer))
    weights.append(fetch(query_w, qw_v, 7))
    weights.append(fetch(key_w, kw_v, 8))
    weights.append(fetch(weight, weight_v, 10))

    width = table.shape[0]
    places = width // 4
    spread = (
        lax.broadcasted_iota(jnp.int32, (places, width), 1) // 4
        == lax.broadcasted_iota(jnp.int32, (places, width), 0)
    ).astype(BF16)
    letter = (lax.broadcasted_iota(jnp.int32, (1, width), 1) % 4).astype(F32)

    def one_hot(start, rows):
        codes = base_v[pl.ds(start, rows), :].astype(F32).astype(BF16)
        wide = jnp.dot(codes, spread, preferred_element_type=F32)
        hot[pl.ds(start, rows), :] = jnp.where(wide == letter, 1.0, 0.0).astype(BF16)

    def embed(start, rows):
        for col in range(0, channels, 256):
            xs[pl.ds(start, rows), pl.ds(col, 256)] = jnp.dot(
                hot[pl.ds(start, rows), :],
                table_v[:, pl.ds(col, 256)],
                preferred_element_type=F32,
            )

    own.wait()
    one_hot(HALO, slab)
    pl.semaphore_wait(barrier, n - 1)
    to_right = pltpu.make_async_remote_copy(
        src_ref=bases.at[pl.ds(slab - HALO, HALO)],
        dst_ref=base_v.at[pl.ds(0, HALO)],
        send_sem=halo_send.at[0],
        recv_sem=halo_recv.at[0],
        device_id={"seq": right},
        device_id_type=MESH,
    )
    to_right.start()
    to_left = pltpu.make_async_remote_copy(
        src_ref=bases.at[pl.ds(0, HALO)],
        dst_ref=base_v.at[pl.ds(HALO + slab, HALO)],
        send_sem=halo_send.at[1],
        recv_sem=halo_recv.at[1],
        device_id={"seq": left},
        device_id_type=MESH,
    )
    to_left.start()

    first_row = me * slab - HALO
    last_row = n * slab
    reaches = [2 * s for s in DILATIONS]
    lows = [HALO - sum(reaches[layer + 1 :]) for layer in range(3)]
    scaled = []
    edge = lows[0] + (full // 2 - lows[0]) // 16 * 16 + 32
    blocks = []
    for layer in range(3):
        if layer > 0:
            edge -= reaches[layer]
        blocks.append(((lows[layer], edge - lows[layer]), (edge, full - lows[layer] - edge)))

    def norm_piece(layer, r, rows):
        floats = xs[pl.ds(r, rows), :]
        mean = jnp.sum(floats * floats, axis=1, keepdims=True) * (1.0 / channels)
        scale = lax.rsqrt(mean + 1e-6)
        if r < HALO or r + rows > HALO + slab:
            place = first_row + r + lax.broadcasted_iota(jnp.int32, (rows, 1), 0)
            inside = jnp.logical_and(place >= 0, place < last_row)
            scale = jnp.where(inside, scale, 0.0)
        nrm[layer % 2, pl.ds(r, rows), :] = (floats * scale).astype(BF16)

    def norms(layer, low, rows):
        return [
            functools.partial(norm_piece, layer, r, size) for r, size in pieces_of(low, rows, 32)
        ]

    def conv_piece(layer, r, rows, col):
        s = DILATIONS[layer]
        total = None
        low = (r - 2 * s) // 16 * 16
        span = -(-(r + rows + 2 * s - low) // 16) * 16
        if s % 16:
            near = nrm[layer % 2, pl.ds(low, span), pl.ds(col, 128)]
        for t in range(KW):
            at = r + (t - 2) * s
            if s % 16:
                part = near[at - low : at - low + rows]
            else:
                part = nrm[layer % 2, pl.ds(at, rows), pl.ds(col, 128)]
            term = part * scaled[layer][t : t + 1, col : col + 128]
            total = term if total is None else total + term
        act[layer % 2, pl.ds(r, rows), pl.ds(col, 128)] = gelu_of_half(total)

    def convs(layer, k):
        at, size = blocks[layer][k]
        return [
            functools.partial(conv_piece, layer, r, rows, col)
            for r, rows in pieces_of(at, size, 112)
            for col in range(0, channels, 128)
        ]

    def mix_piece(layer, r, rows, col):
        mixed = xs[pl.ds(r, rows), pl.ds(col, 256)] + jnp.dot(
            act[layer % 2, pl.ds(r, rows), :],
            point_v[layer, :, pl.ds(col, 256)],
            preferred_element_type=F32,
        )
        if layer < 2:
            xs[pl.ds(r, rows), pl.ds(col, 256)] = mixed
        else:
            trunk_v[pl.ds(r - HALO, rows), pl.ds(col, 256)] = mixed.astype(BF16)

    def mixes(layer, k):
        at, size = blocks[layer][k]
        return [
            functools.partial(mix_piece, layer, at, size, col)
            for col in range(0, channels, 256)
        ]

    def next_norms(layer, k):
        if layer == 2:
            return []
        return norms(layer + 1, *blocks[layer][k])

    get_table.wait()
    for at in range(0, slab, slab // 2):
        embed(HALO + at, slab // 2)
    for task in norms(0, HALO, slab):
        task()
    to_right.wait()
    to_left.wait()
    for start in (0, HALO + slab):
        one_hot(start, HALO)
        embed(start, HALO)
    for weight in weights:
        weight.wait()
    for layer in range(3):
        scaled.append((taps_v[:, layer] * (0.5 * gains_v[pl.ds(layer, 1), :])).astype(BF16))
    for task in norms(0, 0, HALO) + norms(0, HALO + slab, HALO):
        task()

    interleave(convs(0, 0), [])
    for layer in range(3):
        interleave(mixes(layer, 0), convs(layer, 1))
        following = convs(layer + 1, 0) if layer < 2 else []
        interleave(mixes(layer, 1), next_norms(layer, 0) + following)
        interleave([], next_norms(layer, 1))

    put_trunk = pltpu.make_async_copy(trunk_v, trunk_out, local_sem.at[9])
    put_trunk.start()
    group = lax.broadcasted_iota(jnp.int32, (pool_rows, slab), 1) // POOL
    pooler = jnp.where(
        group == lax.broadcasted_iota(jnp.int32, (pool_rows, slab), 0), 1.0 / POOL, 0.0
    ).astype(BF16)
    pooled = jnp.dot(pooler, trunk_v[...], preferred_element_type=F32).astype(BF16)
    mine = pl.ds(pl.multiple_of(me * pool_rows, pool_rows), pool_rows)
    keys[mine, :] = jnp.dot(pooled, kw_v[...], preferred_element_type=F32).astype(BF16)

    copies = []
    for d in sorted(range(1, n), key=lambda d: -min(d, n - d)):
        copies.append(
            pltpu.make_async_remote_copy(
                src_ref=keys.at[mine],
                dst_ref=keys.at[mine],
                send_sem=send_sem.at[d - 1],
                recv_sem=recv_sem.at[d - 1],
                device_id={"seq": lax.rem(me + d, n)},
                device_id_type=MESH,
            )
        )
        copies[-1].start()
    own_queries = jnp.dot(pooled, qw_v[...], preferred_element_type=F32).astype(BF16)
    queries[pl.ds(16, pool_rows), :] = own_queries
    for k, (source, target, peer) in enumerate(
        ((pool_rows, 0, right), (16, 16 + pool_rows, left))
    ):
        copies.append(
            pltpu.make_async_remote_copy(
                src_ref=queries.at[pl.ds(source, 16)],
                dst_ref=queries.at[pl.ds(target, 16)],
                send_sem=query_send.at[k],
                recv_sem=query_recv.at[k],
                device_id={"seq": peer},
                device_id_type=MESH,
            )
        )
        copies[-1].start()

    def spread_rows(rows, places):
        short = 128 - rows.shape[0]
        cols = (0.5 * jnp.concatenate([rows, jnp.zeros((short, 128), F32)], axis=0)).T
        for source, target in places:
            qcols[target] = jnp.broadcast_to(cols[:, source : source + 1], (128, 128)).astype(BF16)

    def combine(i):
        for b in range(3):
            weff[i // 2, pl.ds(b * 128, 128), pl.ds(i % 2 * 128, 128)] = (
                qcols[i] * weight_v[0, b]
                + qcols[i + 1] * weight_v[1, b]
                + qcols[i + 2] * weight_v[2, b]
            )

    spread_rows(own_queries.astype(F32), [(i, i + 1) for i in range(pool_rows)])
    for i in range(1, pool_rows - 1):
        combine(i)
    for copy in copies[-2:]:
        copy.wait()
    above = jnp.where(me > 0, queries[0:16, :].astype(F32), 0.0)
    below = jnp.where(me < n - 1, queries[pl.ds(16 + pool_rows, 16), :].astype(F32), 0.0)
    spread_rows(jnp.concatenate([above, below], axis=0), [(15, 0), (16, pool_rows + 1)])
    combine(0)
    combine(pool_rows - 1)
    for copy in copies[:-2]:
        copy.wait()
    put_trunk.wait()


def pair_kernel_body(
    n, block, keys, queries, weff, trunk_in, pair_out, trunk_out, keys3, qrows, trunk_v, sem
):
    step = pl.program_id(0)
    steps = pl.num_programs(0)
    width = keys.shape[0]
    pool_rows = width // n

    @pl.when(step == 0)
    def _():
        pltpu.make_async_copy(trunk_in, trunk_v, sem.at[0]).start()
        floats = keys[...].astype(F32)
        zero = jnp.zeros((1, 128), F32)
        keys3[:, 0:128] = jnp.concatenate([zero, floats[:-1]], axis=0).astype(BF16)
        keys3[:, 128:256] = keys[...]
        keys3[:, 256:384] = jnp.concatenate([floats[1:], zero], axis=0).astype(BF16)
        qrows[...] = queries[pl.ds(16, pool_rows), :].astype(F32)

    for half in range(block // 2):
        base = step * block + half * 2
        conv = jnp.dot(keys3[...], weff[half], preferred_element_type=F32).astype(BF16)
        for k in range(2):
            row = jnp.broadcast_to(qrows[pl.ds(base + k, 1), :], (16, 128)).astype(BF16)
            pair = (keys[...].reshape(width // 16, 16, 128) * row[None]).reshape(width, 128)
            pair_out[half * 2 + k] = pair + gelu_of_half(conv[:, k * 128 : k * 128 + 128])

    @pl.when(step == 0)
    def _():
        pltpu.make_async_copy(trunk_in, trunk_v, sem.at[0]).wait()
        pltpu.make_async_copy(trunk_v, trunk_out, sem.at[1]).start()

    @pl.when(step == steps - 1)
    def _():
        pltpu.make_async_copy(trunk_v, trunk_out, sem.at[1]).wait()


def on_device(
    n, bases, embed_table, norm_gains, depth_taps, point_weight, query_weight, key_weight, pair_kernel
):
    slab = bases.shape[0]
    channels = embed_table.shape[1]
    full = slab + 2 * HALO
    pool_rows = slab // POOL
    width = pool_rows * n
    hbm_spec = pl.BlockSpec(memory_space=pltpu.HBM)
    vmem_spec = pl.BlockSpec(memory_space=pltpu.VMEM)
    trunk, keys, queries, weff = pl.pallas_call(
        functools.partial(trunk_kernel, n),
        out_shape=(
            jax.ShapeDtypeStruct((slab, channels), BF16),
            jax.ShapeDtypeStruct((width, 128), BF16),
            jax.ShapeDtypeStruct((pool_rows + 32, 128), BF16),
            jax.ShapeDtypeStruct((pool_rows // 2, 384, 256), BF16),
        ),
        in_specs=[hbm_spec] * 8,
        out_specs=(hbm_spec, vmem_spec, vmem_spec, vmem_spec),
        scratch_shapes=[
            pltpu.VMEM((full, bases.shape[1]), jnp.int32),
            pltpu.VMEM(embed_table.shape, BF16),
            pltpu.VMEM(norm_gains.shape, F32),
            pltpu.VMEM((KW, 3, channels), F32),
            pltpu.VMEM(point_weight.shape, BF16),
            pltpu.VMEM(query_weight.shape, BF16),
            pltpu.VMEM(key_weight.shape, BF16),
            pltpu.VMEM(pair_kernel.shape, BF16),
            pltpu.VMEM((pool_rows + 2, 128, 128), BF16),
            pltpu.VMEM((full, embed_table.shape[0]), BF16),
            pltpu.VMEM((full, channels), F32),
            pltpu.VMEM((2, full, channels), BF16),
            pltpu.VMEM((2, full, channels), BF16),
            pltpu.VMEM((slab, channels), BF16),
            pltpu.SemaphoreType.DMA((11,)),
            pltpu.SemaphoreType.DMA((2,)),
            pltpu.SemaphoreType.DMA((2,)),
            pltpu.SemaphoreType.DMA((2,)),
            pltpu.SemaphoreType.DMA((2,)),
            pltpu.SemaphoreType.DMA((n - 1,)),
            pltpu.SemaphoreType.DMA((n - 1,)),
        ],
        compiler_params=pltpu.CompilerParams(
            collective_id=0, has_side_effects=True, vmem_limit_bytes=32 * 1024 * 1024
        ),
        name="trunk_and_gather",
    )(
        *(
            pltpu.with_memory_space_constraint(array, pltpu.HBM)
            for array in (
                bases,
                embed_table,
                norm_gains,
                depth_taps.swapaxes(0, 1),
                point_weight,
                query_weight,
                key_weight,
                pair_kernel,
            )
        )
    )

    block = 8
    pair_map, trunk = pl.pallas_call(
        functools.partial(pair_kernel_body, n, block),
        grid=(pool_rows // block,),
        out_shape=(
            jax.ShapeDtypeStruct((pool_rows, width, 128), BF16),
            jax.ShapeDtypeStruct((slab, channels), BF16),
        ),
        in_specs=[
            pl.BlockSpec((width, 128), lambda i: (0, 0)),
            pl.BlockSpec((pool_rows + 32, 128), lambda i: (0, 0)),
            pl.BlockSpec((block // 2, 384, 256), lambda i: (i, 0, 0)),
            hbm_spec,
        ],
        out_specs=(pl.BlockSpec((block, width, 128), lambda i: (i, 0, 0)), hbm_spec),
        scratch_shapes=[
            pltpu.VMEM((width, 384), BF16),
            pltpu.VMEM((pool_rows, 128), F32),
            pltpu.VMEM((slab, channels), BF16),
            pltpu.SemaphoreType.DMA((2,)),
        ],
        compiler_params=pltpu.CompilerParams(vmem_limit_bytes=32 * 1024 * 1024),
        name="pair_map",
    )(keys, queries, weff, trunk)
    return (trunk, pair_map)


def solution(mesh):
    return jax.shard_map(
        functools.partial(on_device, mesh.shape["seq"]),
        mesh=mesh,
        in_specs=(P(("batch", "seq"), None), P(), P(), P(), P(), P(), P(), P()),
        out_specs=(P(("batch", "seq"), None), P(("batch", "seq"), None, None)),
        check_vma=False,
    )
```

```python
import functools

import jax
import jax.numpy as jnp
from jax import lax
from jax.experimental import pallas as pl
from jax.experimental.pallas import tpu as pltpu
from jax.sharding import PartitionSpec as P

KW = 5
DILATIONS = (2, 8, 32)
POOL = 16
HALO = 96
CHUNK = 32
GELU_A = 0.7978845608028654
GELU_B = 0.7978845608028654 * 0.044715
MESH = pl.DeviceIdType.MESH
F32 = jnp.float32
BF16 = jnp.bfloat16


def gelu_of_half(half):
    return half + half * jnp.tanh(half * (2 * GELU_A + 8 * GELU_B * (half * half)))


def pieces_of(low, rows, most):
    return [(low + at, min(most, rows - at)) for at in range(0, rows, most)]


def trunk_kernel(
    n,
    bases,
    table,
    gains,
    taps,
    point,
    query_w,
    key_w,
    weight,
    trunk_out,
    keys,
    queries,
    weff,
    base_v,
    table_v,
    gains_v,
    taps_v,
    point_v,
    qw_v,
    kw_v,
    weight_v,
    qcols,
    scaled,
    hot,
    xs,
    nrm,
    act,
    trunk_v,
    local_sem,
    halo_send,
    halo_recv,
    query_send,
    query_recv,
    send_sem,
    recv_sem,
):
    slab = bases.shape[0]
    channels = table.shape[1]
    full = slab + 2 * HALO
    pool_rows = slab // POOL
    me = lax.axis_index("seq")
    right = lax.rem(me + 1, n)
    left = lax.rem(me + n - 1, n)

    barrier = pltpu.get_barrier_semaphore()
    for d in range(1, n):
        pl.semaphore_signal(
            barrier, inc=1, device_id={"seq": lax.rem(me + d, n)}, device_id_type=MESH
        )

    def fetch(source, target, k):
        copy = pltpu.make_async_copy(source, target, local_sem.at[k])
        copy.start()
        return copy

    own = fetch(bases, base_v.at[pl.ds(HALO, slab)], 0)
    get_table = fetch(table, table_v, 1)
    weights = [fetch(gains, gains_v, 2), fetch(taps, taps_v, 3)]
    for layer in range(3):
        weights.append(fetch(point.at[layer], point_v.at[layer], 4 + layer))
    weights.append(fetch(query_w, qw_v, 7))
    weights.append(fetch(key_w, kw_v, 8))
    weights.append(fetch(weight, weight_v, 10))

    width = table.shape[0]
    places = width // 4
    spread = (
        lax.broadcasted_iota(jnp.int32, (places, width), 1) // 4
        == lax.broadcasted_iota(jnp.int32, (places, width), 0)
    ).astype(BF16)
    letter = (lax.broadcasted_iota(jnp.int32, (1, width), 1) % 4).astype(F32)

    def one_hot(start, rows):
        codes = base_v[pl.ds(start, rows), :].astype(F32).astype(BF16)
        wide = jnp.dot(codes, spread, preferred_element_type=F32)
        hot[pl.ds(start, rows), :] = jnp.where(wide == letter, 1.0, 0.0).astype(BF16)

    def embed(start, rows):
        @pl.loop(0, channels // 256)
        def _(c):
            col = pl.multiple_of(c * 256, 256)
            xs[pl.ds(start, rows), pl.ds(col, 256)] = jnp.dot(
                hot[pl.ds(start, rows), :],
                table_v[:, pl.ds(col, 256)],
                preferred_element_type=F32,
            )

    own.wait()
    one_hot(HALO, slab)
    pl.semaphore_wait(barrier, n - 1)
    to_right = pltpu.make_async_remote_copy(
        src_ref=bases.at[pl.ds(slab - HALO, HALO)],
        dst_ref=base_v.at[pl.ds(0, HALO)],
        send_sem=halo_send.at[0],
        recv_sem=halo_recv.at[0],
        device_id={"seq": right},
        device_id_type=MESH,
    )
    to_right.start()
    to_left = pltpu.make_async_remote_copy(
        src_ref=bases.at[pl.ds(0, HALO)],
        dst_ref=base_v.at[pl.ds(HALO + slab, HALO)],
        send_sem=halo_send.at[1],
        recv_sem=halo_recv.at[1],
        device_id={"seq": left},
        device_id_type=MESH,
    )
    to_left.start()

    first_row = me * slab - HALO
    last_row = n * slab
    reaches = [2 * s for s in DILATIONS]
    lows = [HALO - sum(reaches[layer + 1 :]) for layer in range(3)]
    edge = lows[0] + (full // 2 - lows[0]) // 16 * 16 + 32
    blocks = []
    for layer in range(3):
        if layer > 0:
            edge -= reaches[layer]
        blocks.append(((lows[layer], edge - lows[layer]), (edge, full - lows[layer] - edge)))

    def norm_piece(layer, r, rows):
        floats = xs[pl.ds(r, rows), :]
        mean = jnp.sum(floats * floats, axis=1, keepdims=True) * (1.0 / channels)
        place = first_row + r + lax.broadcasted_iota(jnp.int32, (rows, 1), 0)
        inside = jnp.logical_and(place >= 0, place < last_row)
        scale = jnp.where(inside, lax.rsqrt(mean + 1e-6), 0.0)
        nrm[layer % 2, pl.ds(r, rows), :] = (floats * scale).astype(BF16)

    def norms(layer, low, rows):
        whole = rows // 64

        @pl.loop(0, whole)
        def _(k):
            for part in range(4):
                norm_piece(layer, pl.multiple_of(low + k * 64 + part * 16, 16), 16)

        for at in range(whole * 64, rows, 16):
            norm_piece(layer, pl.multiple_of(low + at, 16), 16)

    def conv_piece(layer, r, rows, col):
        s = DILATIONS[layer]
        total = None
        low = (r - 2 * s) // 16 * 16
        span = -(-(r + rows + 2 * s - low) // 16) * 16
        if s % 16:
            near = nrm[layer % 2, pl.ds(low, span), pl.ds(col, 128)]
        for t in range(KW):
            at = r + (t - 2) * s
            if s % 16:
                part = near[at - low : at - low + rows]
            else:
                part = nrm[layer % 2, pl.ds(at, rows), pl.ds(col, 128)]
            tap = scaled[layer, t, :, pl.ds(col, 128)]
            term = part.reshape(rows // 16, 16, 128) * tap[None]
            total = term if total is None else total + term
        act[layer % 2, pl.ds(r, rows), pl.ds(col, 128)] = gelu_of_half(total).reshape(rows, 128)

    def conv_chunk(layer, k, chunk):
        for half in range(2):
            for r, rows in pieces_of(*blocks[layer][k], 112):
                conv_piece(layer, r, rows, pl.multiple_of(chunk * 256 + half * 128, 128))

    def mix_chunk(layer, k, chunk):
        r, rows = blocks[layer][k]
        col = pl.multiple_of(chunk * 256, 256)
        mixed = xs[pl.ds(r, rows), pl.ds(col, 256)] + jnp.dot(
            act[layer % 2, pl.ds(r, rows), :],
            point_v[layer, :, pl.ds(col, 256)],
            preferred_element_type=F32,
        )
        if layer < 2:
            xs[pl.ds(r, rows), pl.ds(col, 256)] = mixed
        else:
            trunk_v[pl.ds(r - HALO, rows), pl.ds(col, 256)] = mixed.astype(BF16)

    get_table.wait()
    embed(HALO, slab)
    norms(0, HALO, slab)
    to_right.wait()
    to_left.wait()

    @pl.loop(0, 2)
    def _(side):
        start = pl.multiple_of(side * (HALO + slab), 16)
        one_hot(start, HALO)
        embed(start, HALO)
        norms(0, start, HALO)

    for weight_copy in weights:
        weight_copy.wait()
    for layer in range(3):
        for t in range(KW):
            row = taps_v[pl.ds(t, 1), layer, :] * (0.5 * gains_v[pl.ds(layer, 1), :])
            scaled[layer, t] = jnp.broadcast_to(row, (16, channels)).astype(BF16)

    @pl.loop(0, channels // 256)
    def _(chunk):
        conv_chunk(0, 0, chunk)

    for layer in range(3):

        @pl.loop(0, channels // 256)
        def _(chunk, layer=layer):
            mix_chunk(layer, 0, chunk)
            conv_chunk(layer, 1, chunk)

        if layer < 2:
            norms(layer + 1, *blocks[layer][0])

        @pl.loop(0, channels // 256)
        def _(chunk, layer=layer):
            mix_chunk(layer, 1, chunk)
            if layer < 2:
                conv_chunk(layer + 1, 0, chunk)

        if layer < 2:
            norms(layer + 1, *blocks[layer][1])

    put_trunk = pltpu.make_async_copy(trunk_v, trunk_out, local_sem.at[9])
    put_trunk.start()
    group = lax.broadcasted_iota(jnp.int32, (pool_rows, slab), 1) // POOL
    pooler = jnp.where(
        group == lax.broadcasted_iota(jnp.int32, (pool_rows, slab), 0), 1.0 / POOL, 0.0
    ).astype(BF16)
    pooled = jnp.dot(pooler, trunk_v[...], preferred_element_type=F32).astype(BF16)
    mine = pl.ds(pl.multiple_of(me * pool_rows, pool_rows), pool_rows)
    keys[mine, :] = jnp.dot(pooled, kw_v[...], preferred_element_type=F32).astype(BF16)

    copies = []
    for d in sorted(range(1, n), key=lambda d: -min(d, n - d)):
        copies.append(
            pltpu.make_async_remote_copy(
                src_ref=keys.at[mine],
                dst_ref=keys.at[mine],
                send_sem=send_sem.at[d - 1],
                recv_sem=recv_sem.at[d - 1],
                device_id={"seq": lax.rem(me + d, n)},
                device_id_type=MESH,
            )
        )
        copies[-1].start()
    own_queries = jnp.dot(pooled, qw_v[...], preferred_element_type=F32).astype(BF16)
    queries[pl.ds(16, pool_rows), :] = own_queries
    for k, (source, target, peer) in enumerate(
        ((pool_rows, 0, right), (16, 16 + pool_rows, left))
    ):
        copies.append(
            pltpu.make_async_remote_copy(
                src_ref=queries.at[pl.ds(source, 16)],
                dst_ref=queries.at[pl.ds(target, 16)],
                send_sem=query_send.at[k],
                recv_sem=query_recv.at[k],
                device_id={"seq": peer},
                device_id_type=MESH,
            )
        )
        copies[-1].start()

    def spread_rows(rows, places):
        short = 128 - rows.shape[0]
        cols = (0.5 * jnp.concatenate([rows, jnp.zeros((short, 128), F32)], axis=0)).T
        for source, target in places:
            qcols[target] = jnp.broadcast_to(cols[:, source : source + 1], (128, 128)).astype(BF16)

    def combine(pair):
        for k in range(2):
            i = pair * 2 + k
            for b in range(3):
                weff[pair, pl.ds(b * 128, 128), pl.ds(k * 128, 128)] = (
                    qcols[i] * weight_v[0, b]
                    + qcols[i + 1] * weight_v[1, b]
                    + qcols[i + 2] * weight_v[2, b]
                )

    spread_rows(own_queries.astype(F32), [(i, i + 1) for i in range(pool_rows)])

    @pl.loop(1, pool_rows // 2 - 1)
    def _(pair):
        combine(pair)

    for copy in copies[-2:]:
        copy.wait()
    above = jnp.where(me > 0, queries[0:16, :].astype(F32), 0.0)
    below = jnp.where(me < n - 1, queries[pl.ds(16 + pool_rows, 16), :].astype(F32), 0.0)
    spread_rows(jnp.concatenate([above, below], axis=0), [(15, 0), (16, pool_rows + 1)])

    @pl.loop(0, 2)
    def _(end):
        combine(end * (pool_rows // 2 - 1))

    for copy in copies[:-2]:
        copy.wait()
    put_trunk.wait()


def pair_kernel_body(
    n, block, keys, queries, weff, trunk_in, pair_out, trunk_out, keys3, qrows, trunk_v, sem
):
    step = pl.program_id(0)
    steps = pl.num_programs(0)
    width = keys.shape[0]
    pool_rows = width // n

    @pl.when(step == 0)
    def _():
        pltpu.make_async_copy(trunk_in, trunk_v, sem.at[0]).start()
        floats = keys[...].astype(F32)
        zero = jnp.zeros((1, 128), F32)
        keys3[:, 0:128] = jnp.concatenate([zero, floats[:-1]], axis=0).astype(BF16)
        keys3[:, 128:256] = keys[...]
        keys3[:, 256:384] = jnp.concatenate([floats[1:], zero], axis=0).astype(BF16)
        qrows[...] = queries[pl.ds(16, pool_rows), :].astype(F32)

    for half in range(block // 2):
        base = step * block + half * 2
        conv = jnp.dot(keys3[...], weff[half], preferred_element_type=F32).astype(BF16)
        for k in range(2):
            row = jnp.broadcast_to(qrows[pl.ds(base + k, 1), :], (16, 128)).astype(BF16)
            pair = (keys[...].reshape(width // 16, 16, 128) * row[None]).reshape(width, 128)
            pair_out[half * 2 + k] = pair + gelu_of_half(conv[:, k * 128 : k * 128 + 128])

    @pl.when(step == 0)
    def _():
        pltpu.make_async_copy(trunk_in, trunk_v, sem.at[0]).wait()
        pltpu.make_async_copy(trunk_v, trunk_out, sem.at[1]).start()

    @pl.when(step == steps - 1)
    def _():
        pltpu.make_async_copy(trunk_v, trunk_out, sem.at[1]).wait()


def on_device(
    n, bases, embed_table, norm_gains, depth_taps, point_weight, query_weight, key_weight, pair_kernel
):
    slab = bases.shape[0]
    channels = embed_table.shape[1]
    full = slab + 2 * HALO
    pool_rows = slab // POOL
    width = pool_rows * n
    hbm_spec = pl.BlockSpec(memory_space=pltpu.HBM)
    vmem_spec = pl.BlockSpec(memory_space=pltpu.VMEM)
    trunk, keys, queries, weff = pl.pallas_call(
        functools.partial(trunk_kernel, n),
        out_shape=(
            jax.ShapeDtypeStruct((slab, channels), BF16),
            jax.ShapeDtypeStruct((width, 128), BF16),
            jax.ShapeDtypeStruct((pool_rows + 32, 128), BF16),
            jax.ShapeDtypeStruct((pool_rows // 2, 384, 256), BF16),
        ),
        in_specs=[hbm_spec] * 8,
        out_specs=(hbm_spec, vmem_spec, vmem_spec, vmem_spec),
        scratch_shapes=[
            pltpu.VMEM((full, bases.shape[1]), jnp.int32),
            pltpu.VMEM(embed_table.shape, BF16),
            pltpu.VMEM(norm_gains.shape, F32),
            pltpu.VMEM((KW, 3, channels), F32),
            pltpu.VMEM(point_weight.shape, BF16),
            pltpu.VMEM(query_weight.shape, BF16),
            pltpu.VMEM(key_weight.shape, BF16),
            pltpu.VMEM(pair_kernel.shape, BF16),
            pltpu.VMEM((pool_rows + 2, 128, 128), BF16),
            pltpu.VMEM((3, KW, 16, channels), BF16),
            pltpu.VMEM((full, embed_table.shape[0]), BF16),
            pltpu.VMEM((full, channels), F32),
            pltpu.VMEM((2, full, channels), BF16),
            pltpu.VMEM((2, full, channels), BF16),
            pltpu.VMEM((slab, channels), BF16),
            pltpu.SemaphoreType.DMA((11,)),
            pltpu.SemaphoreType.DMA((2,)),
            pltpu.SemaphoreType.DMA((2,)),
            pltpu.SemaphoreType.DMA((2,)),
            pltpu.SemaphoreType.DMA((2,)),
            pltpu.SemaphoreType.DMA((n - 1,)),
            pltpu.SemaphoreType.DMA((n - 1,)),
        ],
        compiler_params=pltpu.CompilerParams(
            collective_id=0, has_side_effects=True, vmem_limit_bytes=32 * 1024 * 1024
        ),
        name="trunk_and_gather",
    )(
        *(
            pltpu.with_memory_space_constraint(array, pltpu.HBM)
            for array in (
                bases,
                embed_table,
                norm_gains,
                depth_taps.swapaxes(0, 1),
                point_weight,
                query_weight,
                key_weight,
                pair_kernel,
            )
        )
    )

    block = 8
    pair_map, trunk = pl.pallas_call(
        functools.partial(pair_kernel_body, n, block),
        grid=(pool_rows // block,),
        out_shape=(
            jax.ShapeDtypeStruct((pool_rows, width, 128), BF16),
            jax.ShapeDtypeStruct((slab, channels), BF16),
        ),
        in_specs=[
            pl.BlockSpec((width, 128), lambda i: (0, 0)),
            pl.BlockSpec((pool_rows + 32, 128), lambda i: (0, 0)),
            pl.BlockSpec((block // 2, 384, 256), lambda i: (i, 0, 0)),
            hbm_spec,
        ],
        out_specs=(pl.BlockSpec((block, width, 128), lambda i: (i, 0, 0)), hbm_spec),
        scratch_shapes=[
            pltpu.VMEM((width, 384), BF16),
            pltpu.VMEM((pool_rows, 128), F32),
            pltpu.VMEM((slab, channels), BF16),
            pltpu.SemaphoreType.DMA((2,)),
        ],
        compiler_params=pltpu.CompilerParams(vmem_limit_bytes=32 * 1024 * 1024),
        name="pair_map",
    )(keys, queries, weff, trunk)
    return (trunk, pair_map)


def solution(mesh):
    return jax.shard_map(
        functools.partial(on_device, mesh.shape["seq"]),
        mesh=mesh,
        in_specs=(P(("batch", "seq"), None), P(), P(), P(), P(), P(), P(), P()),
        out_specs=(P(("batch", "seq"), None), P(("batch", "seq"), None, None)),
        check_vma=False,
    )
```

```python
import functools

import jax
import jax.numpy as jnp
from jax import lax
from jax.experimental import pallas as pl
from jax.experimental.pallas import tpu as pltpu
from jax.sharding import PartitionSpec as P

KW = 5
DILATIONS = (2, 8, 32)
POOL = 16
HALO = 96
CHUNK = 32
GELU_A = 0.7978845608028654
GELU_B = 0.7978845608028654 * 0.044715
MESH = pl.DeviceIdType.MESH
F32 = jnp.float32
BF16 = jnp.bfloat16


def gelu_of_half(half):
    return half + half * jnp.tanh(half * (2 * GELU_A + 8 * GELU_B * (half * half)))


def pieces_of(low, rows, most):
    return [(low + at, min(most, rows - at)) for at in range(0, rows, most)]


def interleave(first, second):
    count = max(len(first), len(second), 1)
    done = [0, 0]
    for k in range(count):
        for which, tasks in enumerate((first, second)):
            target = len(tasks) * (k + 1) // count
            while done[which] < target:
                tasks[done[which]]()
                done[which] += 1


def trunk_kernel(
    n,
    bases,
    table,
    gains,
    taps,
    point,
    query_w,
    key_w,
    weight,
    trunk_out,
    keys,
    queries,
    weff,
    base_v,
    table_v,
    gains_v,
    taps_v,
    point_v,
    qw_v,
    kw_v,
    weight_v,
    qcols,
    hot,
    xs,
    nrm,
    act,
    trunk_v,
    local_sem,
    halo_send,
    halo_recv,
    query_send,
    query_recv,
    send_sem,
    recv_sem,
):
    slab = bases.shape[0]
    channels = table.shape[1]
    full = slab + 2 * HALO
    pool_rows = slab // POOL
    me = lax.axis_index("seq")
    right = lax.rem(me + 1, n)
    left = lax.rem(me + n - 1, n)

    barrier = pltpu.get_barrier_semaphore()
    for d in range(1, n):
        pl.semaphore_signal(
            barrier, inc=1, device_id={"seq": lax.rem(me + d, n)}, device_id_type=MESH
        )

    def fetch(source, target, k):
        copy = pltpu.make_async_copy(source, target, local_sem.at[k])
        copy.start()
        return copy

    own = fetch(bases, base_v.at[pl.ds(2 * HALO, slab)], 0)
    get_table = fetch(table, table_v, 1)
    weights = [fetch(gains, gains_v, 2), fetch(taps, taps_v, 3)]
    for layer in range(3):
        weights.append(fetch(point.at[layer], point_v.at[layer], 4 + layer))
    weights.append(fetch(query_w, qw_v, 7))
    weights.append(fetch(key_w, kw_v, 8))
    weights.append(fetch(weight, weight_v, 10))

    width = table.shape[0]
    places = width // 4
    spread = (
        lax.broadcasted_iota(jnp.int32, (places, width), 1) // 4
        == lax.broadcasted_iota(jnp.int32, (places, width), 0)
    ).astype(BF16)
    letter = (lax.broadcasted_iota(jnp.int32, (1, width), 1) % 4).astype(F32)

    def one_hot(start, rows):
        codes = base_v[pl.ds(start, rows), :].astype(F32).astype(BF16)
        wide = jnp.dot(codes, spread, preferred_element_type=F32)
        hot[pl.ds(start, rows), :] = jnp.where(wide == letter, 1.0, 0.0).astype(BF16)

    def embed(start, rows, places):
        for col in range(0, channels, 256):
            embedded = jnp.dot(
                hot[pl.ds(start, rows), :],
                table_v[:, pl.ds(col, 256)],
                preferred_element_type=F32,
            )
            for source, target, count in places:
                xs[pl.ds(target, count), pl.ds(col, 256)] = embedded[source : source + count]

    own.wait()
    one_hot(2 * HALO, slab)
    pl.semaphore_wait(barrier, n - 1)
    to_right = pltpu.make_async_remote_copy(
        src_ref=bases.at[pl.ds(slab - HALO, HALO)],
        dst_ref=base_v.at[pl.ds(0, HALO)],
        send_sem=halo_send.at[0],
        recv_sem=halo_recv.at[0],
        device_id={"seq": right},
        device_id_type=MESH,
    )
    to_right.start()
    to_left = pltpu.make_async_remote_copy(
        src_ref=bases.at[pl.ds(0, HALO)],
        dst_ref=base_v.at[pl.ds(HALO, HALO)],
        send_sem=halo_send.at[1],
        recv_sem=halo_recv.at[1],
        device_id={"seq": left},
        device_id_type=MESH,
    )
    to_left.start()

    first_row = me * slab - HALO
    last_row = n * slab
    reaches = [2 * s for s in DILATIONS]
    lows = [HALO - sum(reaches[layer + 1 :]) for layer in range(3)]
    scaled = []
    edge = lows[0] + (full // 2 - lows[0]) // 16 * 16 + 32
    blocks = []
    for layer in range(3):
        if layer > 0:
            edge -= reaches[layer]
        blocks.append(((lows[layer], edge - lows[layer]), (edge, full - lows[layer] - edge)))

    def norm_piece(layer, r, rows):
        floats = xs[pl.ds(r, rows), :]
        mean = jnp.sum(floats * floats, axis=1, keepdims=True) * (1.0 / channels)
        scale = lax.rsqrt(mean + 1e-6)
        if r < HALO or r + rows > HALO + slab:
            place = first_row + r + lax.broadcasted_iota(jnp.int32, (rows, 1), 0)
            inside = jnp.logical_and(place >= 0, place < last_row)
            scale = jnp.where(inside, scale, 0.0)
        nrm[layer % 2, pl.ds(r, rows), :] = (floats * scale).astype(BF16)

    def norms(layer, low, rows):
        return [
            functools.partial(norm_piece, layer, r, size) for r, size in pieces_of(low, rows, 32)
        ]

    def conv_piece(layer, r, rows, col):
        s = DILATIONS[layer]
        total = None
        low = (r - 2 * s) // 16 * 16
        span = -(-(r + rows + 2 * s - low) // 16) * 16
        if s % 16:
            near = nrm[layer % 2, pl.ds(low, span), pl.ds(col, 128)]
        for t in range(KW):
            at = r + (t - 2) * s
            if s % 16:
                part = near[at - low : at - low + rows]
            else:
                part = nrm[layer % 2, pl.ds(at, rows), pl.ds(col, 128)]
            term = part * scaled[layer][t : t + 1, col : col + 128]
            total = term if total is None else total + term
        act[layer % 2, pl.ds(r, rows), pl.ds(col, 128)] = gelu_of_half(total)

    def convs(layer, k):
        at, size = blocks[layer][k]
        return [
            functools.partial(conv_piece, layer, r, rows, col)
            for r, rows in pieces_of(at, size, 112)
            for col in range(0, channels, 128)
        ]

    def mix_piece(layer, r, rows, col):
        mixed = xs[pl.ds(r, rows), pl.ds(col, 256)] + jnp.dot(
            act[layer % 2, pl.ds(r, rows), :],
            point_v[layer, :, pl.ds(col, 256)],
            preferred_element_type=F32,
        )
        if layer < 2:
            xs[pl.ds(r, rows), pl.ds(col, 256)] = mixed
        else:
            trunk_v[pl.ds(r - HALO, rows), pl.ds(col, 256)] = mixed.astype(BF16)

    def mixes(layer, k):
        at, size = blocks[layer][k]
        return [
            functools.partial(mix_piece, layer, at, size, col)
            for col in range(0, channels, 256)
        ]

    def next_norms(layer, k):
        if layer == 2:
            return []
        return norms(layer + 1, *blocks[layer][k])

    get_table.wait()
    for at in range(0, slab, slab // 2):
        embed(2 * HALO + at, slab // 2, [(0, HALO + at, slab // 2)])
    for task in norms(0, HALO, slab):
        task()
    to_right.wait()
    to_left.wait()
    one_hot(0, 2 * HALO)
    embed(0, 2 * HALO, [(0, 0, HALO), (HALO, HALO + slab, HALO)])
    for weight in weights:
        weight.wait()
    for layer in range(3):
        scaled.append((taps_v[:, layer] * (0.5 * gains_v[pl.ds(layer, 1), :])).astype(BF16))
    for task in norms(0, 0, HALO) + norms(0, HALO + slab, HALO):
        task()

    interleave(convs(0, 0), [])
    for layer in range(3):
        interleave(mixes(layer, 0), convs(layer, 1))
        following = convs(layer + 1, 0) if layer < 2 else []
        interleave(mixes(layer, 1), next_norms(layer, 0) + following)
        interleave([], next_norms(layer, 1))

    put_trunk = pltpu.make_async_copy(trunk_v, trunk_out, local_sem.at[9])
    put_trunk.start()
    group = lax.broadcasted_iota(jnp.int32, (pool_rows, slab), 1) // POOL
    pooler = jnp.where(
        group == lax.broadcasted_iota(jnp.int32, (pool_rows, slab), 0), 1.0 / POOL, 0.0
    ).astype(BF16)
    pooled = jnp.dot(pooler, trunk_v[...], preferred_element_type=F32).astype(BF16)
    mine = pl.ds(pl.multiple_of(me * pool_rows, pool_rows), pool_rows)
    keys[mine, :] = jnp.dot(pooled, kw_v[...], preferred_element_type=F32).astype(BF16)

    copies = []
    for d in sorted(range(1, n), key=lambda d: -min(d, n - d)):
        copies.append(
            pltpu.make_async_remote_copy(
                src_ref=keys.at[mine],
                dst_ref=keys.at[mine],
                send_sem=send_sem.at[d - 1],
                recv_sem=recv_sem.at[d - 1],
                device_id={"seq": lax.rem(me + d, n)},
                device_id_type=MESH,
            )
        )
        copies[-1].start()
    own_queries = jnp.dot(pooled, qw_v[...], preferred_element_type=F32).astype(BF16)
    queries[pl.ds(16, pool_rows), :] = own_queries
    for k, (source, target, peer) in enumerate(
        ((pool_rows, 0, right), (16, 16 + pool_rows, left))
    ):
        copies.append(
            pltpu.make_async_remote_copy(
                src_ref=queries.at[pl.ds(source, 16)],
                dst_ref=queries.at[pl.ds(target, 16)],
                send_sem=query_send.at[k],
                recv_sem=query_recv.at[k],
                device_id={"seq": peer},
                device_id_type=MESH,
            )
        )
        copies[-1].start()

    def spread_rows(rows, places):
        short = 128 - rows.shape[0]
        cols = (0.5 * jnp.concatenate([rows, jnp.zeros((short, 128), F32)], axis=0)).T
        for source, target in places:
            qcols[target] = jnp.broadcast_to(cols[:, source : source + 1], (128, 128)).astype(BF16)

    def combine(i):
        for b in range(3):
            weff[i // 2, pl.ds(b * 128, 128), pl.ds(i % 2 * 128, 128)] = (
                qcols[i] * weight_v[0, b]
                + qcols[i + 1] * weight_v[1, b]
                + qcols[i + 2] * weight_v[2, b]
            )

    spread_rows(own_queries.astype(F32), [(i, i + 1) for i in range(pool_rows)])
    for i in range(1, pool_rows - 1):
        combine(i)
    for copy in copies[-2:]:
        copy.wait()
    above = jnp.where(me > 0, queries[0:16, :].astype(F32), 0.0)
    below = jnp.where(me < n - 1, queries[pl.ds(16 + pool_rows, 16), :].astype(F32), 0.0)
    spread_rows(jnp.concatenate([above, below], axis=0), [(15, 0), (16, pool_rows + 1)])
    combine(0)
    combine(pool_rows - 1)
    for copy in copies[:-2]:
        copy.wait()
    put_trunk.wait()


def pair_kernel_body(n, keys, queries, weff, trunk_in, pair_out, trunk_out, keys3, made, sem):
    width = keys.shape[0]
    pool_rows = width // n
    pairs = pool_rows // 2

    put_trunk = pltpu.make_async_copy(trunk_in, trunk_out, sem.at[pairs])
    put_trunk.start()
    floats = keys[...].astype(F32)
    zero = jnp.zeros((1, 128), F32)
    keys3[:, 0:128] = jnp.concatenate([zero, floats[:-1]], axis=0).astype(BF16)
    keys3[:, 128:256] = keys[...]
    keys3[:, 256:384] = jnp.concatenate([floats[1:], zero], axis=0).astype(BF16)
    rows = queries[pl.ds(16, pool_rows), :].astype(F32)

    def convolve(i):
        return jnp.dot(keys3[...], weff[i], preferred_element_type=F32).astype(BF16)

    copies = []
    following = convolve(0)
    for i in range(pairs):
        conv = following
        if i + 1 < pairs:
            following = convolve(i + 1)
        for k in range(2):
            at = i * 2 + k
            row = jnp.broadcast_to(rows[at : at + 1], (16, 128)).astype(BF16)
            pair = (keys[...].reshape(width // 16, 16, 128) * row[None]).reshape(width, 128)
            made[at] = pair + gelu_of_half(conv[:, k * 128 : k * 128 + 128])
        copies.append(
            pltpu.make_async_copy(
                made.at[pl.ds(i * 2, 2)], pair_out.at[pl.ds(i * 2, 2)], sem.at[i]
            )
        )
        copies[-1].start()
    for copy in copies:
        copy.wait()
    put_trunk.wait()


def on_device(
    n, bases, embed_table, norm_gains, depth_taps, point_weight, query_weight, key_weight, pair_kernel
):
    slab = bases.shape[0]
    channels = embed_table.shape[1]
    full = slab + 2 * HALO
    pool_rows = slab // POOL
    width = pool_rows * n
    hbm_spec = pl.BlockSpec(memory_space=pltpu.HBM)
    vmem_spec = pl.BlockSpec(memory_space=pltpu.VMEM)
    trunk, keys, queries, weff = pl.pallas_call(
        functools.partial(trunk_kernel, n),
        out_shape=(
            jax.ShapeDtypeStruct((slab, channels), BF16),
            jax.ShapeDtypeStruct((width, 128), BF16),
            jax.ShapeDtypeStruct((pool_rows + 32, 128), BF16),
            jax.ShapeDtypeStruct((pool_rows // 2, 384, 256), BF16),
        ),
        in_specs=[hbm_spec] * 8,
        out_specs=(hbm_spec, vmem_spec, vmem_spec, vmem_spec),
        scratch_shapes=[
            pltpu.VMEM((full, bases.shape[1]), jnp.int32),
            pltpu.VMEM(embed_table.shape, BF16),
            pltpu.VMEM(norm_gains.shape, F32),
            pltpu.VMEM((KW, 3, channels), F32),
            pltpu.VMEM(point_weight.shape, BF16),
            pltpu.VMEM(query_weight.shape, BF16),
            pltpu.VMEM(key_weight.shape, BF16),
            pltpu.VMEM(pair_kernel.shape, BF16),
            pltpu.VMEM((pool_rows + 2, 128, 128), BF16),
            pltpu.VMEM((full, embed_table.shape[0]), BF16),
            pltpu.VMEM((full, channels), F32),
            pltpu.VMEM((2, full, channels), BF16),
            pltpu.VMEM((2, full, channels), BF16),
            pltpu.VMEM((slab, channels), BF16),
            pltpu.SemaphoreType.DMA((11,)),
            pltpu.SemaphoreType.DMA((2,)),
            pltpu.SemaphoreType.DMA((2,)),
            pltpu.SemaphoreType.DMA((2,)),
            pltpu.SemaphoreType.DMA((2,)),
            pltpu.SemaphoreType.DMA((n - 1,)),
            pltpu.SemaphoreType.DMA((n - 1,)),
        ],
        compiler_params=pltpu.CompilerParams(
            collective_id=0, has_side_effects=True, vmem_limit_bytes=32 * 1024 * 1024
        ),
        name="trunk_and_gather",
    )(
        *(
            pltpu.with_memory_space_constraint(array, pltpu.HBM)
            for array in (
                bases,
                embed_table,
                norm_gains,
                depth_taps.swapaxes(0, 1),
                point_weight,
                query_weight,
                key_weight,
                pair_kernel,
            )
        )
    )

    pair_map, trunk = pl.pallas_call(
        functools.partial(pair_kernel_body, n),
        out_shape=(
            jax.ShapeDtypeStruct((pool_rows, width, 128), BF16),
            jax.ShapeDtypeStruct((slab, channels), BF16),
        ),
        in_specs=[vmem_spec] * 4,
        out_specs=(hbm_spec, hbm_spec),
        scratch_shapes=[
            pltpu.VMEM((width, 384), BF16),
            pltpu.VMEM((pool_rows, width, 128), BF16),
            pltpu.SemaphoreType.DMA((pool_rows // 2 + 1,)),
        ],
        compiler_params=pltpu.CompilerParams(vmem_limit_bytes=32 * 1024 * 1024),
        name="pair_map",
    )(keys, queries, weff, trunk)
    return (trunk, pair_map)


def solution(mesh):
    return jax.shard_map(
        functools.partial(on_device, mesh.shape["seq"]),
        mesh=mesh,
        in_specs=(P(("batch", "seq"), None), P(), P(), P(), P(), P(), P(), P()),
        out_specs=(P(("batch", "seq"), None), P(("batch", "seq"), None, None)),
        check_vma=False,
    )
```

```python
import functools

import jax
import jax.numpy as jnp
from jax import lax
from jax.experimental import pallas as pl
from jax.experimental.pallas import tpu as pltpu
from jax.sharding import PartitionSpec as P

KW = 5
DILATIONS = (2, 8, 32)
POOL = 16
HALO = 96
CHUNK = 32
GELU_A = 0.7978845608028654
GELU_B = 0.7978845608028654 * 0.044715
MESH = pl.DeviceIdType.MESH
F32 = jnp.float32
BF16 = jnp.bfloat16


def gelu_of_half(half):
    return half + half * jnp.tanh(half * (2 * GELU_A + 8 * GELU_B * (half * half)))


def pieces_of(low, rows, most):
    return [(low + at, min(most, rows - at)) for at in range(0, rows, most)]


def interleave(first, second):
    count = max(len(first), len(second), 1)
    done = [0, 0]
    for k in range(count):
        for which, tasks in enumerate((first, second)):
            target = len(tasks) * (k + 1) // count
            while done[which] < target:
                tasks[done[which]]()
                done[which] += 1


def trunk_kernel(
    n,
    bases,
    table,
    gains,
    taps,
    point,
    query_w,
    key_w,
    weight,
    trunk_out,
    keys,
    queries,
    weff,
    base_v,
    table_v,
    gains_v,
    taps_v,
    point_v,
    qw_v,
    kw_v,
    weight_v,
    qcols,
    hot,
    xs,
    nrm,
    act,
    trunk_v,
    local_sem,
    halo_send,
    halo_recv,
    query_send,
    query_recv,
    send_sem,
    recv_sem,
):
    slab = bases.shape[0]
    channels = table.shape[1]
    full = slab + 2 * HALO
    pool_rows = slab // POOL
    me = lax.axis_index("seq")
    right = lax.rem(me + 1, n)
    left = lax.rem(me + n - 1, n)

    barrier = pltpu.get_barrier_semaphore()
    for d in range(1, n):
        pl.semaphore_signal(
            barrier, inc=1, device_id={"seq": lax.rem(me + d, n)}, device_id_type=MESH
        )

    def fetch(source, target, k):
        copy = pltpu.make_async_copy(source, target, local_sem.at[k])
        copy.start()
        return copy

    own = fetch(bases, base_v.at[pl.ds(2 * HALO, slab)], 0)
    get_table = fetch(table, table_v, 1)
    weights = [fetch(gains, gains_v, 2), fetch(taps, taps_v, 3)]
    for layer in range(3):
        weights.append(fetch(point.at[layer], point_v.at[layer], 4 + layer))
    weights.append(fetch(query_w, qw_v, 7))
    weights.append(fetch(key_w, kw_v, 8))
    weights.append(fetch(weight, weight_v, 10))

    width = table.shape[0]
    places = width // 4
    spread = (
        lax.broadcasted_iota(jnp.int32, (places, width), 1) // 4
        == lax.broadcasted_iota(jnp.int32, (places, width), 0)
    ).astype(BF16)
    letter = (lax.broadcasted_iota(jnp.int32, (1, width), 1) % 4).astype(F32)

    def one_hot(start, rows):
        codes = base_v[pl.ds(start, rows), :].astype(F32).astype(BF16)
        wide = jnp.dot(codes, spread, preferred_element_type=F32)
        hot[pl.ds(start, rows), :] = jnp.where(wide == letter, 1.0, 0.0).astype(BF16)

    def embed(start, rows, places):
        for col in range(0, channels, 256):
            embedded = jnp.dot(
                hot[pl.ds(start, rows), :],
                table_v[:, pl.ds(col, 256)],
                preferred_element_type=F32,
            )
            for source, target, count in places:
                xs[pl.ds(target, count), pl.ds(col, 256)] = embedded[source : source + count]

    own.wait()
    one_hot(2 * HALO, slab)
    pl.semaphore_wait(barrier, n - 1)
    to_right = pltpu.make_async_remote_copy(
        src_ref=bases.at[pl.ds(slab - HALO, HALO)],
        dst_ref=base_v.at[pl.ds(0, HALO)],
        send_sem=halo_send.at[0],
        recv_sem=halo_recv.at[0],
        device_id={"seq": right},
        device_id_type=MESH,
    )
    to_right.start()
    to_left = pltpu.make_async_remote_copy(
        src_ref=bases.at[pl.ds(0, HALO)],
        dst_ref=base_v.at[pl.ds(HALO, HALO)],
        send_sem=halo_send.at[1],
        recv_sem=halo_recv.at[1],
        device_id={"seq": left},
        device_id_type=MESH,
    )
    to_left.start()

    first_row = me * slab - HALO
    last_row = n * slab
    reaches = [2 * s for s in DILATIONS]
    lows = [HALO - sum(reaches[layer + 1 :]) for layer in range(3)]
    scaled = []
    edge = lows[0] + (full // 2 - lows[0]) // 16 * 16 + 32
    blocks = []
    for layer in range(3):
        if layer > 0:
            edge -= reaches[layer]
        blocks.append(((lows[layer], edge - lows[layer]), (edge, full - lows[layer] - edge)))

    def norm_piece(layer, r, rows):
        floats = xs[pl.ds(r, rows), :]
        mean = jnp.sum(floats * floats, axis=1, keepdims=True) * (1.0 / channels)
        scale = lax.rsqrt(mean + 1e-6)
        if r < HALO or r + rows > HALO + slab:
            place = first_row + r + lax.broadcasted_iota(jnp.int32, (rows, 1), 0)
            inside = jnp.logical_and(place >= 0, place < last_row)
            scale = jnp.where(inside, scale, 0.0)
        nrm[layer % 2, pl.ds(r, rows), :] = (floats * scale).astype(BF16)

    def norms(layer, low, rows):
        return [
            functools.partial(norm_piece, layer, r, size) for r, size in pieces_of(low, rows, 32)
        ]

    def conv_piece(layer, r, rows, col):
        s = DILATIONS[layer]
        total = None
        low = (r - 2 * s) // 16 * 16
        span = -(-(r + rows + 2 * s - low) // 16) * 16
        if s % 16:
            near = nrm[layer % 2, pl.ds(low, span), pl.ds(col, 128)]
        for t in range(KW):
            at = r + (t - 2) * s
            if s % 16:
                part = near[at - low : at - low + rows]
            else:
                part = nrm[layer % 2, pl.ds(at, rows), pl.ds(col, 128)]
            term = part * scaled[layer][t : t + 1, col : col + 128]
            total = term if total is None else total + term
        act[layer % 2, pl.ds(r, rows), pl.ds(col, 128)] = gelu_of_half(total)

    def convs(layer, k):
        at, size = blocks[layer][k]
        return [
            functools.partial(conv_piece, layer, r, rows, col)
            for r, rows in pieces_of(at, size, 112)
            for col in range(0, channels, 128)
        ]

    def mix_piece(layer, r, rows, col):
        mixed = xs[pl.ds(r, rows), pl.ds(col, 256)] + jnp.dot(
            act[layer % 2, pl.ds(r, rows), :],
            point_v[layer, :, pl.ds(col, 256)],
            preferred_element_type=F32,
        )
        if layer < 2:
            xs[pl.ds(r, rows), pl.ds(col, 256)] = mixed
        else:
            trunk_v[pl.ds(r - HALO, rows), pl.ds(col, 256)] = mixed.astype(BF16)

    def mixes(layer, k):
        at, size = blocks[layer][k]
        return [
            functools.partial(mix_piece, layer, at, size, col)
            for col in range(0, channels, 256)
        ]

    def next_norms(layer, k):
        if layer == 2:
            return []
        return norms(layer + 1, *blocks[layer][k])

    get_table.wait()
    for at in range(0, slab, slab // 2):
        embed(2 * HALO + at, slab // 2, [(0, HALO + at, slab // 2)])
    for task in norms(0, HALO, slab):
        task()
    to_right.wait()
    to_left.wait()
    one_hot(0, 2 * HALO)
    embed(0, 2 * HALO, [(0, 0, HALO), (HALO, HALO + slab, HALO)])
    for weight in weights:
        weight.wait()
    for layer in range(3):
        scaled.append((taps_v[:, layer] * (0.5 * gains_v[pl.ds(layer, 1), :])).astype(BF16))
    for task in norms(0, 0, HALO) + norms(0, HALO + slab, HALO):
        task()

    interleave(convs(0, 0), [])
    def pool_part(k):
        at, size = blocks[2][k]
        at -= HALO
        members = (
            lax.broadcasted_iota(jnp.int32, (pool_rows, size), 1) // POOL
            == lax.broadcasted_iota(jnp.int32, (pool_rows, size), 0) - at // POOL
        )
        pooler = jnp.where(members, 1.0 / POOL, 0.0).astype(BF16)
        return jnp.dot(pooler, trunk_v[pl.ds(at, size), :], preferred_element_type=F32)

    for layer in range(3):
        interleave(mixes(layer, 0), convs(layer, 1))
        following = convs(layer + 1, 0) if layer < 2 else []
        if layer == 2:
            first_pooled = pool_part(0)
        interleave(mixes(layer, 1), next_norms(layer, 0) + following)
        interleave([], next_norms(layer, 1))

    put_trunk = pltpu.make_async_copy(trunk_v, trunk_out, local_sem.at[9])
    put_trunk.start()
    pooled = (first_pooled + pool_part(1)).astype(BF16)
    mine = pl.ds(pl.multiple_of(me * pool_rows, pool_rows), pool_rows)
    keys[mine, :] = jnp.dot(pooled, kw_v[...], preferred_element_type=F32).astype(BF16)

    copies = []
    for d in sorted(range(1, n), key=lambda d: -min(d, n - d)):
        copies.append(
            pltpu.make_async_remote_copy(
                src_ref=keys.at[mine],
                dst_ref=keys.at[mine],
                send_sem=send_sem.at[d - 1],
                recv_sem=recv_sem.at[d - 1],
                device_id={"seq": lax.rem(me + d, n)},
                device_id_type=MESH,
            )
        )
        copies[-1].start()
    own_queries = jnp.dot(pooled, qw_v[...], preferred_element_type=F32).astype(BF16)
    queries[pl.ds(16, pool_rows), :] = own_queries
    for k, (source, target, peer) in enumerate(
        ((pool_rows, 0, right), (16, 16 + pool_rows, left))
    ):
        copies.append(
            pltpu.make_async_remote_copy(
                src_ref=queries.at[pl.ds(source, 16)],
                dst_ref=queries.at[pl.ds(target, 16)],
                send_sem=query_send.at[k],
                recv_sem=query_recv.at[k],
                device_id={"seq": peer},
                device_id_type=MESH,
            )
        )
        copies[-1].start()

    def spread_rows(rows, places):
        short = 128 - rows.shape[0]
        cols = (0.5 * jnp.concatenate([rows, jnp.zeros((short, 128), F32)], axis=0)).T
        for source, target in places:
            qcols[target] = jnp.broadcast_to(cols[:, source : source + 1], (128, 128)).astype(BF16)

    def combine(i):
        for b in range(3):
            weff[i // 2, pl.ds(b * 128, 128), pl.ds(i % 2 * 128, 128)] = (
                qcols[i] * weight_v[0, b]
                + qcols[i + 1] * weight_v[1, b]
                + qcols[i + 2] * weight_v[2, b]
            )

    spread_rows(own_queries.astype(F32), [(i, i + 1) for i in range(pool_rows)])
    for i in range(1, pool_rows - 1):
        combine(i)
    for copy in copies[-2:]:
        copy.wait()
    above = jnp.where(me > 0, queries[0:16, :].astype(F32), 0.0)
    below = jnp.where(me < n - 1, queries[pl.ds(16 + pool_rows, 16), :].astype(F32), 0.0)
    spread_rows(jnp.concatenate([above, below], axis=0), [(15, 0), (16, pool_rows + 1)])
    combine(0)
    combine(pool_rows - 1)
    for copy in copies[:-2]:
        copy.wait()
    put_trunk.wait()


def pair_kernel_body(n, keys, queries, weff, trunk_in, pair_out, trunk_out, keys3, made, sem):
    width = keys.shape[0]
    pool_rows = width // n
    pairs = pool_rows // 2

    put_trunk = pltpu.make_async_copy(trunk_in, trunk_out, sem.at[pairs])
    put_trunk.start()
    floats = keys[...].astype(F32)
    zero = jnp.zeros((1, 128), F32)
    keys3[:, 0:128] = jnp.concatenate([zero, floats[:-1]], axis=0).astype(BF16)
    keys3[:, 128:256] = keys[...]
    keys3[:, 256:384] = jnp.concatenate([floats[1:], zero], axis=0).astype(BF16)
    rows = queries[pl.ds(16, pool_rows), :].astype(F32)

    def convolve(i):
        return jnp.dot(keys3[...], weff[i], preferred_element_type=F32).astype(BF16)

    copies = []
    following = convolve(0)
    for i in range(pairs):
        conv = following
        if i + 1 < pairs:
            following = convolve(i + 1)
        for k in range(2):
            at = i * 2 + k
            row = jnp.broadcast_to(rows[at : at + 1], (16, 128)).astype(BF16)
            pair = (keys[...].reshape(width // 16, 16, 128) * row[None]).reshape(width, 128)
            made[at] = pair + gelu_of_half(conv[:, k * 128 : k * 128 + 128])
        copies.append(
            pltpu.make_async_copy(
                made.at[pl.ds(i * 2, 2)], pair_out.at[pl.ds(i * 2, 2)], sem.at[i]
            )
        )
        copies[-1].start()
    for copy in copies:
        copy.wait()
    put_trunk.wait()


def on_device(
    n, bases, embed_table, norm_gains, depth_taps, point_weight, query_weight, key_weight, pair_kernel
):
    slab = bases.shape[0]
    channels = embed_table.shape[1]
    full = slab + 2 * HALO
    pool_rows = slab // POOL
    width = pool_rows * n
    hbm_spec = pl.BlockSpec(memory_space=pltpu.HBM)
    vmem_spec = pl.BlockSpec(memory_space=pltpu.VMEM)
    trunk, keys, queries, weff = pl.pallas_call(
        functools.partial(trunk_kernel, n),
        out_shape=(
            jax.ShapeDtypeStruct((slab, channels), BF16),
            jax.ShapeDtypeStruct((width, 128), BF16),
            jax.ShapeDtypeStruct((pool_rows + 32, 128), BF16),
            jax.ShapeDtypeStruct((pool_rows // 2, 384, 256), BF16),
        ),
        in_specs=[hbm_spec] * 8,
        out_specs=(hbm_spec, vmem_spec, vmem_spec, vmem_spec),
        scratch_shapes=[
            pltpu.VMEM((full, bases.shape[1]), jnp.int32),
            pltpu.VMEM(embed_table.shape, BF16),
            pltpu.VMEM(norm_gains.shape, F32),
            pltpu.VMEM((KW, 3, channels), F32),
            pltpu.VMEM(point_weight.shape, BF16),
            pltpu.VMEM(query_weight.shape, BF16),
            pltpu.VMEM(key_weight.shape, BF16),
            pltpu.VMEM(pair_kernel.shape, BF16),
            pltpu.VMEM((pool_rows + 2, 128, 128), BF16),
            pltpu.VMEM((full, embed_table.shape[0]), BF16),
            pltpu.VMEM((full, channels), F32),
            pltpu.VMEM((2, full, channels), BF16),
            pltpu.VMEM((2, full, channels), BF16),
            pltpu.VMEM((slab, channels), BF16),
            pltpu.SemaphoreType.DMA((11,)),
            pltpu.SemaphoreType.DMA((2,)),
            pltpu.SemaphoreType.DMA((2,)),
            pltpu.SemaphoreType.DMA((2,)),
            pltpu.SemaphoreType.DMA((2,)),
            pltpu.SemaphoreType.DMA((n - 1,)),
            pltpu.SemaphoreType.DMA((n - 1,)),
        ],
        compiler_params=pltpu.CompilerParams(
            collective_id=0, has_side_effects=True, vmem_limit_bytes=32 * 1024 * 1024
        ),
        name="trunk_and_gather",
    )(
        *(
            pltpu.with_memory_space_constraint(array, pltpu.HBM)
            for array in (
                bases,
                embed_table,
                norm_gains,
                depth_taps.swapaxes(0, 1),
                point_weight,
                query_weight,
                key_weight,
                pair_kernel,
            )
        )
    )

    pair_map, trunk = pl.pallas_call(
        functools.partial(pair_kernel_body, n),
        out_shape=(
            jax.ShapeDtypeStruct((pool_rows, width, 128), BF16),
            jax.ShapeDtypeStruct((slab, channels), BF16),
        ),
        in_specs=[vmem_spec] * 4,
        out_specs=(hbm_spec, hbm_spec),
        scratch_shapes=[
            pltpu.VMEM((width, 384), BF16),
            pltpu.VMEM((pool_rows, width, 128), BF16),
            pltpu.SemaphoreType.DMA((pool_rows // 2 + 1,)),
        ],
        compiler_params=pltpu.CompilerParams(vmem_limit_bytes=32 * 1024 * 1024),
        name="pair_map",
    )(keys, queries, weff, trunk)
    return (trunk, pair_map)


def solution(mesh):
    return jax.shard_map(
        functools.partial(on_device, mesh.shape["seq"]),
        mesh=mesh,
        in_specs=(P(("batch", "seq"), None), P(), P(), P(), P(), P(), P(), P()),
        out_specs=(P(("batch", "seq"), None), P(("batch", "seq"), None, None)),
        check_vma=False,
    )
```
